256 devices in a mesh: tissue: 64 (over x, z, core), chan: 4 (over y).
Axes of the slice: x: 4, y: 4, z: 8, core: 2. Of those that a mesh axis runs over, the one named last changes fastest.
Arguments:
- feats: bfloat16 [768, 8192], P('chan', 'tissue'), may hold values from -6 to 6
- gate_in: bfloat16 [768, 8192], P('chan', 'tissue'), may hold values from -6 to 6
- conv_weight: float32 [9, 768], P(None, 'chan'), may hold values from -2 to 2
- conv_bias: float32 [768], P('chan'), may hold values from 0 to 2
- xproj_weight: bfloat16 [768, 320], P('chan'), may hold values from -1 to 1
- dtproj_weight: bfloat16 [4, 48, 768], P(None, None, 'chan'), may hold values from -3 to 3
- dt_bias: float32 [4, 768], P(None, 'chan'), may hold values from -6 to -2
- a_log: float32 [4, 768, 16], P(None, 'chan'), may hold values from -7 to 3
- skip_gain: float32 [4, 768], P(None, 'chan'), may hold values from 0.5 to 1.5
- row_start: int32 [64], P('tissue'), may hold values from 0 to 31
- row_len: int32 [64], P('tissue'), may hold values from 64 to 96
Outputs:
- gated_out: bfloat16 [768, 8192], P('chan', 'tissue')
The draws below stay inside these ranges and needn't reach their ends.
Inputs may be any that keep to these rules, and one draw needn't show every extreme that they name: row_start + row_len <= 128 in every row.
All inputs are finite; a program needn't handle non-finite values.
Results may differ from the reference program's by a relative error of at most 0.0061.
Values may be sent and summed in bfloat16 or wider, within the bound.
A program may use at most 128 MiB of HBM per device.

```python
import jax
import jax.numpy as jnp
from jax import lax

CH = 768
STATE = 16
RANK = 48
GRID_H = 64
GRID_W = 128
TOKENS = 8192


def draw_conv_bias(key, part):
    key = jax.random.fold_in(key, 5)
    values = jax.random.uniform(key, (CH,), jnp.float32, 0.3, 1.2)
    return values.astype(jnp.float32)


def draw_xproj_weight(key, part):
    key = jax.random.fold_in(key, 11)
    width = 4 * (RANK + 2 * STATE)
    noise = jnp.clip(jax.random.normal(key, (CH, width), jnp.float32), -4.0, 4.0)
    column = jnp.arange(width, dtype=jnp.int32) % (RANK + 2 * STATE)
    offset = jnp.where(column < RANK, 1.5 / CH, 0.0).astype(jnp.float32)
    return (noise * CH ** (-0.5) + offset[None, :]).astype(jnp.bfloat16)


def draw_dtproj_weight(key, part):
    key = jax.random.fold_in(key, 17)
    noise = jnp.clip(jax.random.normal(key, (4, RANK, CH), jnp.float32), -4.0, 4.0)
    offset = 4.0
    return (noise * RANK ** (-0.5) - offset / RANK).astype(jnp.bfloat16)


def with_ends(drawn, rng, smallest, high):
    longest = drawn.shape.index(max(drawn.shape))
    spots = []
    for shift in (0, 1):
        where = [jax.random.randint(jax.random.fold_in(rng, axis), (), 0, length) for axis, length in enumerate(drawn.shape)]
        where[longest] = (where[longest] + shift) % drawn.shape[longest]
        spots.append(tuple(where))
    return drawn.at[spots[0]].set(smallest).at[spots[1]].set(high)


def block_levels(rng, extent, shards, low, high):
    loudness = 1.0
    for dim, shards_of in shards:
        heights = jax.random.uniform(jax.random.fold_in(jax.random.fold_in(rng, 6), dim), (shards_of,), jnp.float32, low / len(shards), high / len(shards))
        loudness = loudness * jnp.repeat(jnp.exp(heights), extent[dim] // shards_of).reshape((-1,) + (1,) * (len(extent) - 1 - dim))
    return loudness


def gaussian(stream_key, dims, deviation, bound, cuts=(), kind=jnp.bfloat16):
    values = deviation * jax.random.normal(stream_key, dims, jnp.float32)
    if cuts:
        values = values * block_levels(stream_key, dims, cuts, -0.22, 0.18)
    return jnp.clip(values, -bound, bound).astype(kind)


def setup_inputs(seed: int = 0) -> dict:
    arg_keys = jax.random.split(jax.random.key(seed), 12)
    feats = gaussian(arg_keys[0], (CH, TOKENS), 1.0, 6.0, ((0, 4), (1, 64)))
    gate_in = gaussian(arg_keys[1], (CH, TOKENS), 1.0, 6.0, ((0, 4), (1, 64)))
    conv_weight = gaussian(arg_keys[2], (9, CH), 0.35, 2.0, ((1, 4),), jnp.float32)
    conv_bias = draw_conv_bias(jax.random.fold_in(arg_keys[11], 71), 0)
    xproj_weight = draw_xproj_weight(jax.random.fold_in(arg_keys[11], 71), 0)
    dtproj_weight = draw_dtproj_weight(jax.random.fold_in(arg_keys[11], 71), 0)
    dt_bias = jnp.clip(-6.0 + 4.0 * jax.random.uniform(arg_keys[6], (4, CH), jnp.float32) ** block_levels(arg_keys[6], (4, CH), ((1, 4),), -0.2, 0.2), -6.0, -2.0)
    a_log = jnp.clip(-7.0 + 10.0 * jax.random.uniform(arg_keys[7], (4, CH, STATE), jnp.float32) ** block_levels(arg_keys[7], (4, CH, STATE), ((1, 4),), -0.2, 0.2), -7.0, 3.0)
    skip_gain = jnp.clip(0.5 + 1.0 * jax.random.uniform(arg_keys[8], (4, CH), jnp.float32) ** block_levels(arg_keys[8], (4, CH), ((1, 4),), -0.2, 0.2), 0.5, 1.5)
    row_start = with_ends(jax.random.randint(arg_keys[9], (GRID_H,), 0, GRID_W // 4), jax.random.fold_in(arg_keys[9], 1), 0, (GRID_W // 4) - 1).astype(jnp.int32)
    row_len = with_ends(jax.random.randint(arg_keys[10], (GRID_H,), GRID_W // 2, 3 * GRID_W // 4 + 1), jax.random.fold_in(arg_keys[10], 1), GRID_W // 2, (3 * GRID_W // 4 + 1) - 1).astype(jnp.int32)
    return dict(feats=feats, gate_in=gate_in, conv_weight=conv_weight, conv_bias=conv_bias, xproj_weight=xproj_weight, dtproj_weight=dtproj_weight, dt_bias=dt_bias, a_log=a_log, skip_gain=skip_gain, row_start=row_start, row_len=row_len)


def to_columns(array):
    return jnp.transpose(array.reshape(GRID_H, GRID_W, -1), (1, 0, 2)).reshape(TOKENS, -1)


def from_columns(array):
    return jnp.transpose(array.reshape(GRID_W, GRID_H, -1), (1, 0, 2)).reshape(TOKENS, -1)


def run_scan(sequence, decay_rates):
    def advance(state_now, inputs):
        step_size, inner_f, in_gate, out_gate = inputs
        state_now = jnp.exp(step_size[:, None] * decay_rates) * state_now + (step_size * inner_f)[:, None] * in_gate[None, :]
        return state_now, jnp.sum(state_now * out_gate[None, :], axis=1)

    _, result = lax.scan(advance, jnp.zeros((CH, STATE), jnp.float32), sequence)
    return result


def reference(feats, gate_in, conv_weight, conv_bias, xproj_weight, dtproj_weight, dt_bias, a_log, skip_gain, row_start, row_len):
    feats = feats.T
    gate_in = gate_in.T
    proj_width = RANK + 2 * STATE
    col_ids = jnp.arange(GRID_W, dtype=jnp.int32)
    tissue_mask = ((col_ids[None, :] >= row_start[:, None]) & (col_ids[None, :] < (row_start + row_len)[:, None])).astype(jnp.float32)
    masked_grid = feats.reshape(GRID_H, GRID_W, CH).astype(jnp.float32) * tissue_mask[:, :, None]
    padded = jnp.pad(masked_grid, ((1, 1), (1, 1), (0, 0)))
    conv_sum = conv_bias + jnp.zeros((GRID_H, GRID_W, CH), jnp.float32)
    for shift_r in range(3):
        for shift_c in range(3):
            conv_sum = conv_sum + conv_weight[shift_r * 3 + shift_c] * padded[shift_r:shift_r + GRID_H, shift_c:shift_c + GRID_W]
    inner = (jax.nn.silu(conv_sum) * tissue_mask[:, :, None]).astype(jnp.bfloat16).reshape(TOKENS, CH)
    projected = jnp.dot(inner, xproj_weight, preferred_element_type=jnp.float32).astype(jnp.bfloat16).reshape(TOKENS, 4, proj_width)
    decay_rates = -jnp.exp(a_log)
    flat_mask = tissue_mask.reshape(TOKENS)
    inner_f = inner.astype(jnp.float32)
    summed = jnp.zeros((TOKENS, CH), jnp.float32)
    for direction in range(4):
        proj_piece = projected[:, direction]
        pre_act = jnp.dot(proj_piece[:, :RANK], dtproj_weight[direction], preferred_element_type=jnp.float32).astype(jnp.bfloat16)
        step_size = flat_mask[:, None] * jax.nn.softplus(pre_act.astype(jnp.float32) + dt_bias[direction])
        in_gate = proj_piece[:, RANK:RANK + STATE].astype(jnp.float32)
        out_gate = proj_piece[:, RANK + STATE:].astype(jnp.float32)
        sequence = (step_size, inner_f, in_gate, out_gate)
        if direction % 2 == 1:
            sequence = tuple(to_columns(array) for array in sequence)
        if direction >= 2:
            sequence = tuple(jnp.flip(array, 0) for array in sequence)
        result = run_scan(sequence, decay_rates[direction])
        if direction >= 2:
            result = jnp.flip(result, 0)
        if direction % 2 == 1:
            result = from_columns(result)
        summed = summed + result + skip_gain[direction] * inner_f
    return (summed * jax.nn.silu(gate_in.astype(jnp.float32))).astype(jnp.bfloat16).T
```

```python
import jax
import jax.numpy as jnp
from jax import lax
from jax.experimental import pallas as pl
from jax.experimental.pallas import tpu as pltpu
from jax.sharding import PartitionSpec as P

MESH = pl.DeviceIdType.MESH
F32 = jnp.float32
BF16 = jnp.bfloat16
PEERS = 64
TEAM = 4
LEN = 128
CHAN = 192
WIDE = 256
STATE = 16
RANK = 48
GROUP = 2 * (RANK + 2 * STATE)
PACK = 2 * CHAN
STEPS = 16
LOG2E = 1.4426950408889634


def nn(a, b):
    return lax.dot_general(a, b, (((1,), (0,)), ((), ())), preferred_element_type=F32)


def nt(a, b):
    return lax.dot_general(a, b, (((1,), (1,)), ((), ())), preferred_element_type=F32)


def token_of(place):
    return lax.rem(place, 8) * STEPS + lax.div(place, 8)


def iota(shape, dim):
    return lax.broadcasted_iota(jnp.int32, shape, dim)


def one_hot(shape, equal):
    return jnp.where(equal(iota(shape, 0), iota(shape, 1)), 1.0, 0.0).astype(BF16)


def silu(v):
    return v / (1.0 + jnp.exp(-v))


def body_kernel(
    feats, gate, conv_w, conv_b, xproj, dtproj, dt_bias, a_log, skip, row_start, row_len,
    out,
    rows3, convp, xw, part, part_in, dtw, bias, decay, skips, aug,
    step, drive, proj, hexc, local, cc, carry_p,
    send_a, recv_a, send_b, recv_b, send_h, recv_h, send_c, recv_c, send_y, recv_y,
    inner_s, yrow, ycol, spare,
    ssem, rsem,
):
    me = lax.axis_index("tissue")
    team = lax.axis_index("chan")

    barrier = pltpu.get_barrier_semaphore()

    def greet(k, _):
        pl.semaphore_signal(barrier, inc=1, device_id=(lax.rem(me + k, PEERS), team), device_id_type=MESH)
        return _

    lax.fori_loop(1, PEERS, greet, 0)
    for k in range(1, TEAM):
        pl.semaphore_signal(barrier, inc=1, device_id=(me, lax.rem(team + k, TEAM)), device_id_type=MESH)

    first, width = row_start[0], row_len[0]
    cols = iota((CHAN, LEN), 1)
    lane_mask = (cols >= first) & (cols < first + width)
    rows3[:, CHAN:, :] = jnp.zeros((3, WIDE - CHAN, LEN), BF16)
    rows3[1, 0:CHAN, :] = jnp.where(lane_mask, feats[...], jnp.zeros((), BF16))

    pl.semaphore_wait(barrier, PEERS - 1 + TEAM - 1)

    below = lax.rem(me + 1, PEERS)
    above = lax.rem(me + PEERS - 1, PEERS)
    halo = [
        pltpu.make_async_remote_copy(
            src_ref=rows3.at[1, pl.ds(0, CHAN)], dst_ref=rows3.at[slot, pl.ds(0, CHAN)],
            send_sem=ssem.at[slot], recv_sem=rsem.at[slot], device_id=(peer, team), device_id_type=MESH,
        )
        for slot, peer in ((0, below), (2, above))
    ]
    for copy in halo:
        copy.start()

    shifts = one_hot((3 * LEN, LEN), lambda r, t: t == token_of(lax.rem(r, LEN)) + lax.div(r, LEN) - 1)
    convp[...] = jnp.zeros_like(convp)
    convp[0:9, 0:CHAN] = conv_w[...]
    convp[9:10, 0:CHAN] = conv_b[...]
    bias[...] = jnp.zeros_like(bias)
    bias[0:4, 0:CHAN] = dt_bias[...]
    skips[...] = jnp.zeros_like(skips)
    skips[0:1, 0:CHAN] = jnp.sum(skip[...], axis=0, keepdims=True)
    aug[...] = jnp.zeros_like(aug)

    def feature(row):
        group, f = lax.div(row, GROUP), lax.rem(row, GROUP)
        low = f < 2 * RANK
        g = f - 2 * RANK
        second = jnp.where(low, lax.div(f, RANK), lax.div(g, 2 * STATE))
        inside = jnp.where(low, lax.rem(f, RANK), RANK + lax.rem(g, 2 * STATE))
        direction = 2 * second + 1 - group
        return direction * (RANK + 2 * STATE) + inside

    order = one_hot((2 * GROUP, 2 * GROUP), lambda r, f: f == feature(r))
    xw[...] = jnp.zeros_like(xw)
    xw[:, 0:CHAN] = nt(order, xproj[...]).astype(BF16)

    dtw[...] = jnp.zeros_like(dtw)
    for d in range(4):
        pair, second = 1 - d % 2, d // 2
        dtw[pair, RANK * second : RANK * second + RANK, WIDE * second : WIDE * second + CHAN] = dtproj[d]
    decay[...] = jnp.zeros_like(decay)
    for d in range(4):
        decay[d, :, 0:CHAN] = -LOG2E * jnp.exp(a_log[d].T)

    def conv_terms(i, source):
        x = nt(shifts, source)
        total = None
        for j in range(3):
            term = convp[3 * i + j : 3 * i + j + 1, :] * x[j * LEN : (j + 1) * LEN]
            total = term if total is None else total + term
        return total

    conv_sum = convp[9:10, :] + conv_terms(1, rows3[1])
    token_rows = token_of(iota((LEN, WIDE), 0))
    row_mask = jnp.where((token_rows >= first) & (token_rows < first + width), 1.0, 0.0)

    halo[0].wait_recv()
    conv_sum = conv_sum + jnp.where(me > 0, 1.0, 0.0) * conv_terms(0, rows3[0])
    halo[1].wait_recv()
    conv_sum = conv_sum + jnp.where(me < PEERS - 1, 1.0, 0.0) * conv_terms(2, rows3[2])
    inner = (silu(conv_sum) * row_mask).astype(BF16)
    inner_s[...] = inner

    def part_copy(group, k):
        sem = 4 + 3 * group + k - 1
        return pltpu.make_async_remote_copy(
            src_ref=part.at[group], dst_ref=part_in.at[group, k - 1],
            send_sem=ssem.at[sem], recv_sem=rsem.at[sem],
            device_id=(me, lax.rem(team + k, TEAM)), device_id_type=MESH,
        )

    own = []
    for group in range(2):
        own.append(nt(xw[group * GROUP : (group + 1) * GROUP, :], inner))
        part[group] = own[group].astype(BF16)
        for k in range(1, TEAM):
            part_copy(group, k).start()

    def exchange(sem, src, dst, slot_there):
        def one(k, _):
            peer = lax.rem(me + k, PEERS)
            pltpu.make_async_remote_copy(
                src_ref=src.at[pl.ds(slot_there(me, peer)[0], 1)], dst_ref=dst.at[pl.ds(slot_there(me, peer)[1], 1)],
                send_sem=ssem.at[sem], recv_sem=rsem.at[sem], device_id=(peer, team), device_id_type=MESH,
            ).start()
            return _

        lax.fori_loop(1, PEERS, one, 0)
        here, there = slot_there(me, me)
        own_row = src.at[pl.ds(here, 1)]
        pltpu.make_async_copy(own_row, dst.at[pl.ds(there, 1)], rsem.at[sem]).start()
        pltpu.make_async_copy(own_row, spare.at[pl.ds(sem - 10, 1), pl.ds(0, src.shape[1])], ssem.at[sem]).start()

    def all_rows(sem, src, dst):
        return pltpu.make_async_remote_copy(
            src_ref=src, dst_ref=dst,
            send_sem=ssem.at[sem], recv_sem=rsem.at[sem], device_id=(below, team), device_id_type=MESH,
        )

    plain = lambda src, dst: (dst, src)

    places = [
        one_hot((WIDE, PACK), lambda e, l, b=b: (l == CHAN * b + e) & (e < CHAN)) for b in range(2)
    ]
    pick_cols = [one_hot((PEERS, LEN), lambda j, p, b=b: token_of(p) == 2 * j + b) for b in range(2)]
    put_cols = [one_hot((LEN, PEERS), lambda p, j, b=b: token_of(p) == 2 * j + b) for b in range(2)]
    pick_rows = [one_hot((PEERS, LEN), lambda r, p, b=b: token_of(p) == PEERS * b + r) for b in range(2)]
    put_rows = [one_hot((LEN, PEERS), lambda p, r, b=b: token_of(p) == PEERS * b + r) for b in range(2)]

    def pack(picked):
        return nn(picked[0].astype(BF16), places[0]) + nn(picked[1].astype(BF16), places[1])

    def unpack(message, puts):
        message = message.astype(BF16)
        return nn(puts[0], nt(message, places[0]).astype(BF16)) + nn(puts[1], nt(message, places[1]).astype(BF16))

    send_a[...] = pack([nn(pick_cols[b], inner) for b in range(2)])
    exchange(10, send_a, recv_a, plain)

    def projected(group):
        total = own[group]
        for k in range(1, TEAM):
            part_copy(group, k).wait_recv()
            total = total + part_in[group, k - 1].astype(F32)
        return total.astype(BF16)

    aug[0, 0:GROUP, :] = projected(0)
    place_lane = iota((16, LEN), 1)
    token_lane = token_of(place_lane)
    aug[0, GROUP : GROUP + 16, :] = jnp.where((token_lane >= first) & (token_lane < first + width), 1.0, 0.0).astype(BF16)
    send_b[...] = pack([nt(pick_cols[b], aug[0]) for b in range(2)])
    exchange(11, send_b, recv_b, plain)

    aug[1, 0:GROUP, :] = projected(1)
    identity = one_hot((LEN, LEN), lambda r, c: r == c)
    sub = iota((8, WIDE), 0)

    def prepare(pair, features, inner_b, mask_b):
        proj[pair] = features
        pre = nn(features[:, 0:LEN].astype(BF16), dtw[1 - pair])
        for second in range(2):
            d = 2 * second + pair
            v = pre[:, WIDE * second : WIDE * second + WIDE].astype(BF16).astype(F32) + bias[d : d + 1, :]
            size = mask_b * (jnp.maximum(v, 0.0) + jnp.log1p(jnp.exp(-jnp.abs(v))))
            step[d] = size
            drive[d] = size * inner_b

    def at(q, second):
        p = STEPS - 1 - q if second else q
        return pl.multiple_of(p * 8, 8)

    def gates(pair, second, rows):
        base = 2 * RANK + 2 * STATE * second
        tile = proj[pair, pl.ds(rows, 8), :]
        ins = [jnp.broadcast_to(tile[:, base + n : base + n + 1], (8, WIDE)) for n in range(STATE)]
        outs = [jnp.broadcast_to(tile[:, base + STATE + n : base + STATE + n + 1], (8, WIDE)) for n in range(STATE)]
        return ins, outs

    def roll_on(x, s, second, fill):
        moved = pltpu.roll(x, 8 - s if second else s, 0)
        keep = sub < 8 - s if second else sub >= s
        return jnp.where(keep, moved, fill)

    def totals(pair):
        for second in range(2):
            d = 2 * second + pair

            def advance(q, carry):
                rows = at(q, second)
                size, push = step[d, pl.ds(rows, 8), :], drive[d, pl.ds(rows, 8), :]
                ins, _ = gates(pair, second, rows)
                new = []
                for n in range(STATE):
                    now = jnp.exp2(decay[d, n : n + 1, :] * size)
                    new.append(now * carry[n] + push * ins[n])
                return tuple(new) + (carry[STATE] + size,)

            zero = jnp.zeros((8, WIDE), F32)
            ends = lax.fori_loop(0, STEPS, advance, (zero,) * (STATE + 1))
            run = ends[STATE]
            for s in (1, 2, 4):
                run = run + roll_on(run, s, second, 0.0)
            carry_p[d] = roll_on(run, 1, second, 0.0)
            end = 0 if second else 7
            for n in range(STATE):
                h, p = ends[n], jnp.exp2(decay[d, n : n + 1, :] * ends[STATE])
                for s in (1, 2, 4):
                    h = p * roll_on(h, s, second, 0.0) + h
                    if s < 4:
                        p = p * roll_on(p, s, second, 1.0)
                hexc[d, 8 * n : 8 * n + 8, :] = roll_on(h, 1, second, 0.0)
                for half in range(2):
                    k = 32 * second + 16 * half + n
                    send_h[pair, k : k + 1, 0:LEN] = h[end : end + 1, LEN * half : LEN * half + LEN]
            whole = jnp.exp2(decay[d] * run[end : end + 1, :])
            for half in range(2):
                k = 32 * second + 16 * half
                send_h[pair, k : k + STATE, LEN : 2 * LEN] = whole[:, LEN * half : LEN * half + LEN]

    def place_in_order(source, owner):
        return jnp.where(owner < PEERS // 2, source, PEERS - 1 - source)

    def send_totals(pair):
        exchange(
            12 + pair, send_h.at[pair], recv_h.at[pair], lambda src, dst: (dst, place_in_order(src, dst))
        )

    def own_scan(pair):
        all_rows(12 + pair, send_h.at[pair], recv_h.at[pair]).wait_recv()
        h, p = recv_h[pair, :, 0:LEN], recv_h[pair, :, LEN : 2 * LEN]
        row = iota((PEERS, LEN), 0)
        for s in (1, 2, 4, 8, 16, 32):
            keep = row >= s
            h = p * jnp.where(keep, pltpu.roll(h, s, 0), 0.0) + h
            if s < 32:
                p = p * jnp.where(keep, pltpu.roll(p, s, 0), 1.0)
        send_c[pair] = jnp.where(row >= 1, pltpu.roll(h, 1, 0), 0.0)
        exchange(
            14 + pair, send_c.at[pair], recv_c.at[pair], lambda src, dst: (place_in_order(dst, src), src)
        )

    def local_pass(pair):
        for second in range(2):
            d = 2 * second + pair

            def advance(q, carry):
                rows = at(q, second)
                size, push = step[d, pl.ds(rows, 8), :], drive[d, pl.ds(rows, 8), :]
                ins, outs = gates(pair, second, rows)
                since = carry[STATE] + size
                new, y = [], jnp.zeros((8, WIDE), F32)
                for n in range(STATE):
                    rate = decay[d, n : n + 1, :]
                    h = jnp.exp2(rate * size) * carry[n] + push * ins[n]
                    y = y + outs[n] * h
                    cc[d, pl.ds(rows * STATE + 8 * n, 8), :] = outs[n] * jnp.exp2(rate * since)
                    new.append(h)
                local[d, pl.ds(rows, 8), :] = y
                return tuple(new) + (since,)

            lax.fori_loop(
                0, STEPS, advance,
                tuple(hexc[d, 8 * n : 8 * n + 8, :] for n in range(STATE)) + (carry_p[d],),
            )

    def finish(pair, dst):
        all_rows(14 + pair, send_c.at[pair], recv_c.at[pair]).wait_recv()

        def advance(p, _):
            rows = pl.multiple_of(p * 8, 8)
            for half in range(2):
                lanes = slice(LEN * half, LEN * half + LEN)
                y = local[pair, pl.ds(rows, 8), lanes] + local[2 + pair, pl.ds(rows, 8), lanes]
                for second in range(2):
                    for n in range(STATE):
                        k = 32 * second + 16 * half + n
                        y = y + cc[2 * second + pair, pl.ds(rows * STATE + 8 * n, 8), lanes] * recv_c[pair, k : k + 1, :]
                dst[pl.ds(rows, 8), lanes] = y
            return _

        lax.fori_loop(0, STEPS, advance, 0)

    inner_f = inner.astype(F32)
    prepare(0, nt(identity, aug[1]), inner_f, row_mask)
    totals(0)
    send_totals(0)

    all_rows(10, send_a, recv_a).wait_recv()
    col_inner = unpack(recv_a[...], put_rows)
    all_rows(11, send_b, recv_b).wait_recv()
    col_feat = unpack(recv_b[...], put_rows)
    prepare(1, col_feat, col_inner, jnp.broadcast_to(col_feat[:, GROUP : GROUP + 1], (LEN, WIDE)))
    totals(1)
    send_totals(1)
    own_scan(0)
    local_pass(1)
    own_scan(1)
    local_pass(0)
    finish(1, ycol)
    back = ycol[...].astype(BF16)
    send_y[...] = pack([nn(pick_rows[b], back) for b in range(2)])
    exchange(16, send_y, recv_y, plain)
    finish(0, yrow)
    natural = one_hot((LEN, LEN), lambda p, t: token_of(p) == t)
    gate_rows = nt(natural, gate[...])
    gated = silu(gate_rows)
    base = yrow[:, 0:CHAN] + skips[0:1, 0:CHAN] * inner_s[:, 0:CHAN].astype(F32)
    all_rows(16, send_y, recv_y).wait_recv()
    summed = base + unpack(recv_y[...], put_cols)[:, 0:CHAN]
    result = (summed * gated).astype(BF16)
    out[...] = lax.dot_general(
        result, natural, (((0,), (0,)), ((), ())), preferred_element_type=F32
    ).astype(BF16)

    for copy in halo:
        copy.wait_send()
    for group in range(2):
        for k in range(1, TEAM):
            part_copy(group, k).wait_send()
    all_rows(10, send_a, recv_a).wait_send()
    all_rows(11, send_b, recv_b).wait_send()
    for pair in range(2):
        all_rows(12 + pair, send_h.at[pair], recv_h.at[pair]).wait_send()
        all_rows(14 + pair, send_c.at[pair], recv_c.at[pair]).wait_send()
    all_rows(16, send_y, recv_y).wait_send()


def body(
    feats, gate_in, conv_weight, conv_bias, xproj_weight, dtproj_weight, dt_bias, a_log, skip_gain, row_start, row_len
):
    vmem = pl.BlockSpec(memory_space=pltpu.VMEM)
    smem = pl.BlockSpec(memory_space=pltpu.SMEM)
    scratch = [
        ((3, WIDE, LEN), BF16),
        ((16, WIDE), F32),
        ((2 * GROUP, WIDE), BF16),
        ((2, GROUP, LEN), BF16),
        ((2, TEAM - 1, GROUP, LEN), BF16),
        ((2, LEN, 2 * WIDE), BF16),
        ((8, WIDE), F32),
        ((4, STATE, WIDE), F32),
        ((8, WIDE), F32),
        ((2, WIDE, LEN), BF16),
        ((4, LEN, WIDE), F32),
        ((4, LEN, WIDE), F32),
        ((2, LEN, WIDE), F32),
        ((4, STATE * 8, WIDE), F32),
        ((4, LEN, WIDE), F32),
        ((4, LEN * STATE, WIDE), F32),
        ((4, 8, WIDE), F32),
        ((PEERS, PACK), F32), ((PEERS, PACK), F32),
        ((PEERS, PACK), F32), ((PEERS, PACK), F32),
        ((2, PEERS, WIDE), F32), ((2, PEERS, WIDE), F32),
        ((2, PEERS, LEN), F32), ((2, PEERS, LEN), F32),
        ((PEERS, PACK), F32), ((PEERS, PACK), F32),
        ((LEN, WIDE), BF16),
        ((LEN, WIDE), F32), ((LEN, WIDE), F32),
        ((8, PACK), F32),
    ]
    return pl.pallas_call(
        body_kernel,
        out_shape=jax.ShapeDtypeStruct((CHAN, LEN), BF16),
        in_specs=[vmem] * 9 + [smem] * 2,
        out_specs=vmem,
        scratch_shapes=[pltpu.VMEM(s, t) for s, t in scratch]
        + [pltpu.SemaphoreType.DMA((17,)), pltpu.SemaphoreType.DMA((17,))],
        compiler_params=pltpu.CompilerParams(
            collective_id=0, has_side_effects=True, vmem_limit_bytes=48 * 1024 * 1024
        ),
    )(
        feats, gate_in, conv_weight, conv_bias.reshape(1, CHAN), xproj_weight, dtproj_weight, dt_bias, a_log,
        skip_gain, row_start, row_len,
    )


def solution(mesh):
    in_specs = (
        P("chan", "tissue"),
        P("chan", "tissue"),
        P(None, "chan"),
        P("chan"),
        P("chan", None),
        P(None, None, "chan"),
        P(None, "chan"),
        P(None, "chan", None),
        P(None, "chan"),
        P("tissue"),
        P("tissue"),
    )
    return jax.shard_map(body, mesh=mesh, in_specs=in_specs, out_specs=P("chan", "tissue"), check_vma=False)
```

```python
import jax
import jax.numpy as jnp
from jax import lax
from jax.experimental import pallas as pl
from jax.experimental.pallas import tpu as pltpu
from jax.sharding import PartitionSpec as P

MESH = pl.DeviceIdType.MESH
F32 = jnp.float32
BF16 = jnp.bfloat16
PEERS = 64
TEAM = 4
LEN = 128
CHAN = 192
WIDE = 256
STATE = 16
RANK = 48
GROUP = 2 * (RANK + 2 * STATE)
PACK = 2 * CHAN
STEPS = 16
LOG2E = 1.4426950408889634


def nn(a, b):
    return lax.dot_general(a, b, (((1,), (0,)), ((), ())), preferred_element_type=F32)


def nt(a, b):
    return lax.dot_general(a, b, (((1,), (1,)), ((), ())), preferred_element_type=F32)


def tn(a, b):
    return lax.dot_general(a, b, (((0,), (0,)), ((), ())), preferred_element_type=F32)


def token_of(place):
    return (place & 7) * STEPS + (place >> 3)


def iota(shape, dim):
    return lax.broadcasted_iota(jnp.int32, shape, dim)


def one_hot(shape, equal):
    return jnp.where(equal(iota(shape, 0), iota(shape, 1)), 1.0, 0.0).astype(BF16)


def silu(v):
    return v / (1.0 + jnp.exp(-v))


def body_kernel(
    feats_hbm, gate_hbm, conv_w_hbm, conv_b_hbm, xproj_hbm, dtproj_hbm, dt_bias_hbm, a_log_hbm, skip_hbm, start_hbm, len_hbm,
    out,
    feats, gate, conv_w, conv_b, xproj, dtproj, dt_bias, a_log, skip, row_start, row_len,
    rows3, convp, xw, part, part_in, dtw, bias, decay, skips, aug,
    step, drive, proj, hexc, local, cc, carry_p,
    send_a, recv_a, send_b, recv_b, send_h, recv_h, send_c, recv_c, send_y, recv_y,
    inner_s, yrow, ycol, spare,
    ssem, rsem, isem,
):
    me = lax.axis_index("tissue")
    team = lax.axis_index("chan")

    barrier = pltpu.get_barrier_semaphore()

    def greet(k, _):
        pl.semaphore_signal(barrier, inc=1, device_id=(lax.rem(me + k, PEERS), team), device_id_type=MESH)
        return _

    lax.fori_loop(1, PEERS, greet, 0)
    for k in range(1, TEAM):
        pl.semaphore_signal(barrier, inc=1, device_id=(me, lax.rem(team + k, TEAM)), device_id_type=MESH)

    loads = [
        pltpu.make_async_copy(src, dst, isem.at[n])
        for n, (src, dst) in enumerate((
            (start_hbm, row_start), (len_hbm, row_len), (feats_hbm, feats), (xproj_hbm, xproj), (conv_w_hbm, conv_w),
            (conv_b_hbm, conv_b), (dtproj_hbm, dtproj), (dt_bias_hbm, dt_bias), (a_log_hbm, a_log), (skip_hbm, skip),
            (gate_hbm, gate),
        ))
    ]
    for load in loads:
        load.start()
    rows3[:, CHAN:, :] = jnp.zeros((3, WIDE - CHAN, LEN), BF16)
    for load in loads:
        load.wait()

    first, width = row_start[0], row_len[0]
    cols = iota((CHAN, LEN), 1)
    lane_mask = (cols >= first) & (cols < first + width)
    rows3[1, 0:CHAN, :] = jnp.where(lane_mask, feats[...], jnp.zeros((), BF16))

    shifts = one_hot((3 * LEN, LEN), lambda r, t: t == token_of(r & (LEN - 1)) + (r >> 7) - 1)
    convp[...] = jnp.zeros_like(convp)
    convp[0:9, 0:CHAN] = conv_w[...]
    convp[9:10, 0:CHAN] = conv_b[...]
    bias[...] = jnp.zeros_like(bias)
    bias[0:4, 0:CHAN] = dt_bias[...]
    skips[...] = jnp.zeros_like(skips)
    skips[0:1, 0:CHAN] = jnp.sum(skip[...], axis=0, keepdims=True)
    aug[...] = jnp.zeros_like(aug)

    turned = nt(one_hot((2 * GROUP, 2 * GROUP), lambda r, f: r == f), xproj[...]).astype(BF16)
    xw[...] = jnp.zeros_like(xw)
    for d in range(4):
        top, start = GROUP * (1 - d % 2), (RANK + 2 * STATE) * d
        low, gat = top + RANK * (d // 2), top + 2 * RANK + 2 * STATE * (d // 2)
        xw[low : low + RANK, 0:CHAN] = turned[start : start + RANK]
        xw[gat : gat + 2 * STATE, 0:CHAN] = turned[start + RANK : start + RANK + 2 * STATE]

    dtw[...] = jnp.zeros_like(dtw)
    for d in range(4):
        pair, second = 1 - d % 2, d // 2
        dtw[pair, RANK * second : RANK * second + RANK, WIDE * second : WIDE * second + CHAN] = dtproj[d]
    decay[...] = jnp.zeros_like(decay)
    for d in range(4):
        decay[d, :, 0:CHAN] = -LOG2E * jnp.exp(a_log[d])

    pl.semaphore_wait(barrier, PEERS - 1 + TEAM - 1)

    below = lax.rem(me + 1, PEERS)
    above = lax.rem(me + PEERS - 1, PEERS)
    halo = [
        pltpu.make_async_remote_copy(
            src_ref=rows3.at[1, pl.ds(0, CHAN)], dst_ref=rows3.at[slot, pl.ds(0, CHAN)],
            send_sem=ssem.at[slot], recv_sem=rsem.at[slot], device_id=(peer, team), device_id_type=MESH,
        )
        for slot, peer in ((0, below), (2, above))
    ]
    for copy in halo:
        copy.start()

    def conv_terms(i, source):
        x = nt(shifts, source)
        total = None
        for j in range(3):
            term = convp[3 * i + j : 3 * i + j + 1, :] * x[j * LEN : (j + 1) * LEN]
            total = term if total is None else total + term
        return total

    conv_sum = convp[9:10, :] + conv_terms(1, rows3[1])
    token_rows = token_of(iota((LEN, WIDE), 0))
    row_mask = jnp.where((token_rows >= first) & (token_rows < first + width), 1.0, 0.0)

    halo[0].wait_recv()
    conv_sum = conv_sum + jnp.where(me > 0, 1.0, 0.0) * conv_terms(0, rows3[0])
    halo[1].wait_recv()
    conv_sum = conv_sum + jnp.where(me < PEERS - 1, 1.0, 0.0) * conv_terms(2, rows3[2])
    inner = (silu(conv_sum) * row_mask).astype(BF16)
    inner_s[...] = inner

    def part_copy(group, k):
        sem = 4 + 3 * group + k - 1
        return pltpu.make_async_remote_copy(
            src_ref=part.at[group], dst_ref=part_in.at[group, k - 1],
            send_sem=ssem.at[sem], recv_sem=rsem.at[sem],
            device_id=(me, lax.rem(team + k, TEAM)), device_id_type=MESH,
        )

    own = []
    for group in range(2):
        own.append(nt(xw[group * GROUP : (group + 1) * GROUP, :], inner))
        part[group] = own[group].astype(BF16)
        for k in range(1, TEAM):
            part_copy(group, k).start()

    def exchange(sem, src, dst, slot_there):
        def one(k, _):
            peer = lax.rem(me + k, PEERS)
            pltpu.make_async_remote_copy(
                src_ref=src.at[pl.ds(slot_there(me, peer)[0], 1)], dst_ref=dst.at[pl.ds(slot_there(me, peer)[1], 1)],
                send_sem=ssem.at[sem], recv_sem=rsem.at[sem], device_id=(peer, team), device_id_type=MESH,
            ).start()
            return _

        lax.fori_loop(1, PEERS, one, 0)
        here, there = slot_there(me, me)
        own_row = src.at[pl.ds(here, 1)]
        pltpu.make_async_copy(own_row, dst.at[pl.ds(there, 1)], rsem.at[sem]).start()
        pltpu.make_async_copy(own_row, spare.at[pl.ds(sem - 10, 1), pl.ds(0, src.shape[1])], ssem.at[sem]).start()
        due[sem] = all_rows(sem, src, dst)
        sent.append(due[sem])

    def arrive(sem):
        due.pop(sem).wait_recv()

    sent = list(halo)
    due = {}

    def all_rows(sem, src, dst):
        return pltpu.make_async_remote_copy(
            src_ref=src, dst_ref=dst,
            send_sem=ssem.at[sem], recv_sem=rsem.at[sem], device_id=(below, team), device_id_type=MESH,
        )

    plain = lambda src, dst: (dst, src)

    places = [
        one_hot((WIDE, PACK), lambda e, l, b=b: (l == CHAN * b + e) & (e < CHAN)) for b in range(2)
    ]
    pick_cols = [one_hot((PEERS, LEN), lambda j, p, b=b: token_of(p) == 2 * j + b) for b in range(2)]
    put_cols = [one_hot((LEN, PEERS), lambda p, j, b=b: token_of(p) == 2 * j + b) for b in range(2)]
    pick_rows = [one_hot((PEERS, LEN), lambda r, p, b=b: token_of(p) == PEERS * b + r) for b in range(2)]
    put_rows = [one_hot((LEN, PEERS), lambda p, r, b=b: token_of(p) == PEERS * b + r) for b in range(2)]

    def pack(picked):
        return nn(picked[0].astype(BF16), places[0]) + nn(picked[1].astype(BF16), places[1])

    def unpack(message, puts):
        message = message.astype(BF16)
        return nn(puts[0], nt(message, places[0]).astype(BF16)) + nn(puts[1], nt(message, places[1]).astype(BF16))

    send_a[...] = pack([nn(pick_cols[b], inner) for b in range(2)])
    exchange(10, send_a, recv_a, plain)

    def projected(group):
        total = own[group]
        for k in range(1, TEAM):
            part_copy(group, k).wait_recv()
            total = total + part_in[group, k - 1].astype(F32)
        return total.astype(BF16)

    aug[0, 0:GROUP, :] = projected(0)
    place_lane = iota((16, LEN), 1)
    token_lane = token_of(place_lane)
    aug[0, GROUP : GROUP + 16, :] = jnp.where((token_lane >= first) & (token_lane < first + width), 1.0, 0.0).astype(BF16)
    send_b[...] = pack([nt(pick_cols[b], aug[0]) for b in range(2)])
    exchange(11, send_b, recv_b, plain)

    aug[1, 0:GROUP, :] = projected(1)
    identity = one_hot((LEN, LEN), lambda r, c: r == c)
    sub = iota((8, WIDE), 0)

    def prepare(pair, features, inner_b, mask_b):
        proj[pair] = features
        pre = nn(features[:, 0:LEN].astype(BF16), dtw[1 - pair])
        for second in range(2):
            d = 2 * second + pair
            v = pre[:, WIDE * second : WIDE * second + WIDE].astype(BF16).astype(F32) + bias[d : d + 1, :]
            size = mask_b * (jnp.maximum(v, 0.0) + jnp.log1p(jnp.exp(-jnp.abs(v))))
            step[d] = size
            drive[d] = size * inner_b

    def at(q, second):
        p = STEPS - 1 - q if second else q
        return pl.multiple_of(p * 8, 8)

    def gates(pair, second, rows):
        base = 2 * RANK + 2 * STATE * second
        tile = proj[pair, pl.ds(rows, 8), :]
        ins = [jnp.broadcast_to(tile[:, base + n : base + n + 1], (8, WIDE)) for n in range(STATE)]
        outs = [jnp.broadcast_to(tile[:, base + STATE + n : base + STATE + n + 1], (8, WIDE)) for n in range(STATE)]
        return ins, outs

    def roll_on(x, s, second, fill):
        moved = pltpu.roll(x, 8 - s if second else s, 0)
        keep = sub < 8 - s if second else sub >= s
        return jnp.where(keep, moved, fill)

    def totals(pair):
        part_states = STATE // 2
        zero = jnp.zeros((8, WIDE), F32)
        ends = {}
        for base in range(0, STATE, part_states):

            def advance(q, carry):
                new = []
                for second in range(2):
                    d, rows = 2 * second + pair, at(q, second)
                    size, push = step[d, pl.ds(rows, 8), :], drive[d, pl.ds(rows, 8), :]
                    tile = proj[pair, pl.ds(rows, 8), :]
                    lane = 2 * RANK + 2 * STATE * second + base
                    for n in range(part_states):
                        now = jnp.exp2(decay[d, base + n : base + n + 1, :] * size)
                        gate_in = jnp.broadcast_to(tile[:, lane + n : lane + n + 1], (8, WIDE))
                        new.append(now * carry[part_states * second + n] + push * gate_in)
                return tuple(new)

            got = lax.fori_loop(0, STEPS, advance, (zero,) * (2 * part_states), unroll=4)
            for second in range(2):
                for n in range(part_states):
                    ends[second, base + n] = got[part_states * second + n]
        for second in range(2):
            d = 2 * second + pair
            chunk = step[d, 0:8, :]
            for q in range(1, STEPS):
                chunk = chunk + step[d, 8 * q : 8 * q + 8, :]
            run = chunk
            for s in (1, 2, 4):
                run = run + roll_on(run, s, second, 0.0)
            carry_p[d] = roll_on(run, 1, second, 0.0)
            end = 0 if second else 7
            for n in range(STATE):
                h, p = ends[second, n], jnp.exp2(decay[d, n : n + 1, :] * chunk)
                for s in (1, 2, 4):
                    h = p * roll_on(h, s, second, 0.0) + h
                    if s < 4:
                        p = p * roll_on(p, s, second, 1.0)
                hexc[d, 8 * n : 8 * n + 8, :] = roll_on(h, 1, second, 0.0)
                for half in range(2):
                    k = 32 * second + 16 * half + n
                    send_h[pair, k : k + 1, 0:LEN] = h[end : end + 1, LEN * half : LEN * half + LEN]
            whole = jnp.exp2(decay[d] * run[end : end + 1, :])
            for half in range(2):
                k = 32 * second + 16 * half
                send_h[pair, k : k + STATE, LEN : 2 * LEN] = whole[:, LEN * half : LEN * half + LEN]

    def place_in_order(source, owner):
        return jnp.where(owner < PEERS // 2, source, PEERS - 1 - source)

    def send_totals(pair):
        exchange(
            12 + pair, send_h.at[pair], recv_h.at[pair], lambda src, dst: (dst, place_in_order(src, dst))
        )

    def own_scan(pair):
        arrive(12 + pair)
        h, p = recv_h[pair, :, 0:LEN], recv_h[pair, :, LEN : 2 * LEN]
        row = iota((PEERS, LEN), 0)
        for s in (1, 2, 4, 8, 16, 32):
            keep = row >= s
            h = p * jnp.where(keep, pltpu.roll(h, s, 0), 0.0) + h
            if s < 32:
                p = p * jnp.where(keep, pltpu.roll(p, s, 0), 1.0)
        send_c[pair] = jnp.where(row >= 1, pltpu.roll(h, 1, 0), 0.0)
        exchange(
            14 + pair, send_c.at[pair], recv_c.at[pair], lambda src, dst: (place_in_order(dst, src), src)
        )

    def local_pass(pair):
        for second in range(2):
            d = 2 * second + pair

            def advance(q, carry):
                rows = at(q, second)
                size, push = step[d, pl.ds(rows, 8), :], drive[d, pl.ds(rows, 8), :]
                ins, outs = gates(pair, second, rows)
                since = carry[STATE] + size
                new, y = [], jnp.zeros((8, WIDE), F32)
                for n in range(STATE):
                    rate = decay[d, n : n + 1, :]
                    h = jnp.exp2(rate * size) * carry[n] + push * ins[n]
                    y = y + outs[n] * h
                    cc[d, pl.ds(rows * STATE + 8 * n, 8), :] = outs[n] * jnp.exp2(rate * since)
                    new.append(h)
                local[d, pl.ds(rows, 8), :] = y
                return tuple(new) + (since,)

            lax.fori_loop(
                0, STEPS, advance,
                tuple(hexc[d, 8 * n : 8 * n + 8, :] for n in range(STATE)) + (carry_p[d],),
            )

    def finish(pair, dst):
        arrive(14 + pair)

        def advance(p, _):
            rows = pl.multiple_of(p * 8, 8)
            for half in range(2):
                lanes = slice(LEN * half, LEN * half + LEN)
                y = local[pair, pl.ds(rows, 8), lanes] + local[2 + pair, pl.ds(rows, 8), lanes]
                for second in range(2):
                    for n in range(STATE):
                        k = 32 * second + 16 * half + n
                        y = y + cc[2 * second + pair, pl.ds(rows * STATE + 8 * n, 8), lanes] * recv_c[pair, k : k + 1, :]
                dst[pl.ds(rows, 8), lanes] = y
            return _

        lax.fori_loop(0, STEPS, advance, 0)

    inner_f = inner.astype(F32)
    prepare(0, nt(identity, aug[1]), inner_f, row_mask)
    totals(0)
    send_totals(0)

    arrive(10)
    col_inner = unpack(recv_a[...], put_rows)
    arrive(11)
    col_feat = unpack(recv_b[...], put_rows)
    prepare(1, col_feat, col_inner, jnp.broadcast_to(col_feat[:, GROUP : GROUP + 1], (LEN, WIDE)))
    totals(1)
    send_totals(1)
    own_scan(0)
    local_pass(1)
    own_scan(1)
    local_pass(0)
    finish(1, ycol)
    back = ycol[...].astype(BF16)
    send_y[...] = pack([nn(pick_rows[b], back) for b in range(2)])
    exchange(16, send_y, recv_y, plain)
    finish(0, yrow)
    natural = one_hot((LEN, LEN), lambda p, t: token_of(p) == t)
    base = yrow[...] + skips[0:1, :] * inner_s[...].astype(F32)
    high = base.astype(BF16)
    base = (tn(high, natural) + tn((base - high.astype(F32)).astype(BF16), natural))[0:CHAN]
    gated = silu(gate[...].astype(F32))
    arrive(16)
    back = recv_y[...].astype(BF16)
    spots = [one_hot((PEERS, LEN), lambda j, t, b=b: t == 2 * j + b) for b in range(2)]
    returned = tn(back, spots[0])[0:CHAN] + tn(back, spots[1])[CHAN:PACK]
    out[...] = ((base + returned) * gated).astype(BF16)

    for copy in sent:
        copy.wait_send()
    for group in range(2):
        for k in range(1, TEAM):
            part_copy(group, k).wait_send()


def body(
    feats, gate_in, conv_weight, conv_bias, xproj_weight, dtproj_weight, dt_bias, a_log, skip_gain, row_start, row_len
):
    vmem = pl.BlockSpec(memory_space=pltpu.VMEM)
    hbm = pl.BlockSpec(memory_space=pltpu.HBM)
    inputs = [
        ((CHAN, LEN), BF16), ((CHAN, LEN), BF16), ((9, CHAN), F32), ((1, CHAN), F32), ((CHAN, 2 * GROUP), BF16),
        ((4, RANK, CHAN), BF16), ((4, CHAN), F32), ((4, STATE, CHAN), F32), ((4, CHAN), F32),
    ]
    scratch = [
        ((3, WIDE, LEN), BF16),
        ((16, WIDE), F32),
        ((2 * GROUP, WIDE), BF16),
        ((2, GROUP, LEN), BF16),
        ((2, TEAM - 1, GROUP, LEN), BF16),
        ((2, LEN, 2 * WIDE), BF16),
        ((8, WIDE), F32),
        ((4, STATE, WIDE), F32),
        ((8, WIDE), F32),
        ((2, WIDE, LEN), BF16),
        ((4, LEN, WIDE), F32),
        ((4, LEN, WIDE), F32),
        ((2, LEN, WIDE), F32),
        ((4, STATE * 8, WIDE), F32),
        ((4, LEN, WIDE), F32),
        ((4, LEN * STATE, WIDE), F32),
        ((4, 8, WIDE), F32),
        ((PEERS, PACK), F32), ((PEERS, PACK), F32),
        ((PEERS, PACK), F32), ((PEERS, PACK), F32),
        ((2, PEERS, WIDE), F32), ((2, PEERS, WIDE), F32),
        ((2, PEERS, LEN), F32), ((2, PEERS, LEN), F32),
        ((PEERS, PACK), F32), ((PEERS, PACK), F32),
        ((LEN, WIDE), BF16),
        ((LEN, WIDE), F32), ((LEN, WIDE), F32),
        ((8, PACK), F32),
    ]
    return pl.pallas_call(
        body_kernel,
        out_shape=jax.ShapeDtypeStruct((CHAN, LEN), BF16),
        in_specs=[hbm] * 11,
        out_specs=vmem,
        scratch_shapes=[pltpu.VMEM(s, t) for s, t in inputs] + [pltpu.SMEM((1,), jnp.int32)] * 2
        + [pltpu.VMEM(s, t) for s, t in scratch]
        + [pltpu.SemaphoreType.DMA((17,)), pltpu.SemaphoreType.DMA((17,)), pltpu.SemaphoreType.DMA((11,))],
        compiler_params=pltpu.CompilerParams(
            collective_id=0, has_side_effects=True, vmem_limit_bytes=56 * 1024 * 1024
        ),
    )(
        feats, gate_in, conv_weight, conv_bias.reshape(1, CHAN), xproj_weight, dtproj_weight, dt_bias,
        jnp.swapaxes(a_log, 1, 2), skip_gain, row_start, row_len,
    )


def solution(mesh):
    in_specs = (
        P("chan", "tissue"),
        P("chan", "tissue"),
        P(None, "chan"),
        P("chan"),
        P("chan", None),
        P(None, None, "chan"),
        P(None, "chan"),
        P(None, "chan", None),
        P(None, "chan"),
        P("tissue"),
        P("tissue"),
    )
    return jax.shard_map(body, mesh=mesh, in_specs=in_specs, out_specs=P("chan", "tissue"), check_vma=False)
```

```python
import jax
import jax.numpy as jnp
from jax import lax
from jax.experimental import pallas as pl
from jax.experimental.pallas import tpu as pltpu
from jax.sharding import PartitionSpec as P

MESH = pl.DeviceIdType.MESH
F32 = jnp.float32
BF16 = jnp.bfloat16
PEERS = 64
TEAM = 4
LEN = 128
CHAN = 192
WIDE = 256
STATE = 16
RANK = 48
GROUP = 2 * (RANK + 2 * STATE)
PACK = 2 * CHAN
STEPS = 16
LOG2E = 1.4426950408889634


def nn(a, b):
    return lax.dot_general(a, b, (((1,), (0,)), ((), ())), preferred_element_type=F32)


def nt(a, b):
    return lax.dot_general(a, b, (((1,), (1,)), ((), ())), preferred_element_type=F32)


def tn(a, b):
    return lax.dot_general(a, b, (((0,), (0,)), ((), ())), preferred_element_type=F32)


def token_of(place):
    return (place & 7) * STEPS + (place >> 3)


def iota(shape, dim):
    return lax.broadcasted_iota(jnp.int32, shape, dim)


def one_hot(shape, equal):
    return jnp.where(equal(iota(shape, 0), iota(shape, 1)), 1.0, 0.0).astype(BF16)


def silu(v):
    return v / (1.0 + jnp.exp(-v))


def body_kernel(
    feats_hbm, gate_hbm, conv_w_hbm, conv_b_hbm, xproj_hbm, dtproj_hbm, dt_bias_hbm, a_log_hbm, skip_hbm, start_hbm, len_hbm,
    out,
    feats, gate, conv_w, conv_b, xproj, dtproj, dt_bias, a_log, skip, row_start, row_len,
    rows3, convp, xw, part, part_in, dtw, bias, decay, skips, aug,
    step, drive, proj, hexc, local, cc, carry_p,
    send_a, recv_a, send_b, recv_b, send_h, recv_h, send_c, recv_c, send_y, recv_y,
    inner_s, yrow, ycol, spare,
    ssem, rsem, isem,
):
    me = lax.axis_index("tissue")
    team = lax.axis_index("chan")

    barrier = pltpu.get_barrier_semaphore()

    def away(i):
        q, j = i >> 4, (i >> 1) & 7
        dx = 2 + (q >> 1) - (q & 1) * (1 + 2 * (q >> 1))
        dz = 4 + (j >> 1) - (j & 1) * (1 + 2 * (j >> 1))
        return (((me >> 4) + dx) & 3) * 16 + (((me >> 1) + dz) & 7) * 2 + ((me + i + 1) & 1)

    def greet(i, _):
        pl.semaphore_signal(barrier, inc=1, device_id=(away(i), team), device_id_type=MESH)
        return _

    lax.fori_loop(0, PEERS - 1, greet, 0)
    for k in (2, 1, 3):
        pl.semaphore_signal(barrier, inc=1, device_id=(me, lax.rem(team + k, TEAM)), device_id_type=MESH)

    loads = [
        pltpu.make_async_copy(src, dst, isem.at[n])
        for n, (src, dst) in enumerate((
            (start_hbm, row_start), (len_hbm, row_len), (feats_hbm, feats), (xproj_hbm, xproj), (conv_w_hbm, conv_w),
            (conv_b_hbm, conv_b), (dtproj_hbm, dtproj), (dt_bias_hbm, dt_bias), (a_log_hbm, a_log), (skip_hbm, skip),
            (gate_hbm, gate),
        ))
    ]
    for load in loads:
        load.start()
    rows3[:, CHAN:, :] = jnp.zeros((3, WIDE - CHAN, LEN), BF16)
    for load in loads:
        load.wait()

    first, width = row_start[0, 0], row_len[0, 0]
    cols = iota((CHAN, LEN), 1)
    lane_mask = (cols >= first) & (cols < first + width)
    rows3[1, 0:CHAN, :] = jnp.where(lane_mask, feats[...], jnp.zeros((), BF16))

    shifts = one_hot((3 * LEN, LEN), lambda r, t: t == token_of(r & (LEN - 1)) + (r >> 7) - 1)
    convp[...] = jnp.zeros_like(convp)
    convp[0:9, 0:CHAN] = conv_w[...]
    convp[9:10, 0:CHAN] = conv_b[...]
    bias[...] = jnp.zeros_like(bias)
    bias[0:4, 0:CHAN] = dt_bias[...]
    skips[...] = jnp.zeros_like(skips)
    skips[0:1, 0:CHAN] = jnp.sum(skip[...], axis=0, keepdims=True)
    aug[...] = jnp.zeros_like(aug)

    turned = nt(one_hot((2 * GROUP, 2 * GROUP), lambda r, f: r == f), xproj[...]).astype(BF16)
    xw[...] = jnp.zeros_like(xw)
    for d in range(4):
        top, start = GROUP * (1 - d % 2), (RANK + 2 * STATE) * d
        low, gat = top + RANK * (d // 2), top + 2 * RANK + 2 * STATE * (d // 2)
        xw[low : low + RANK, 0:CHAN] = turned[start : start + RANK]
        xw[gat : gat + 2 * STATE, 0:CHAN] = turned[start + RANK : start + RANK + 2 * STATE]

    dtw[...] = jnp.zeros_like(dtw)
    for d in range(4):
        pair, second = 1 - d % 2, d // 2
        dtw[pair, RANK * second : RANK * second + RANK, WIDE * second : WIDE * second + CHAN] = dtproj[d]
    decay[...] = jnp.zeros_like(decay)
    for d in range(4):
        decay[d, :, 0:CHAN] = -LOG2E * jnp.exp(a_log[d])

    pl.semaphore_wait(barrier, PEERS - 1 + TEAM - 1)

    below = lax.rem(me + 1, PEERS)
    above = lax.rem(me + PEERS - 1, PEERS)
    halo = [
        pltpu.make_async_remote_copy(
            src_ref=rows3.at[1, pl.ds(0, CHAN)], dst_ref=rows3.at[slot, pl.ds(0, CHAN)],
            send_sem=ssem.at[slot], recv_sem=rsem.at[slot], device_id=(peer, team), device_id_type=MESH,
        )
        for slot, peer in ((0, below), (2, above))
    ]
    for copy in halo:
        copy.start()

    def conv_terms(i, source):
        x = nt(shifts, source)
        total = None
        for j in range(3):
            term = convp[3 * i + j : 3 * i + j + 1, :] * x[j * LEN : (j + 1) * LEN]
            total = term if total is None else total + term
        return total

    conv_sum = convp[9:10, :] + conv_terms(1, rows3[1])
    token_rows = token_of(iota((LEN, WIDE), 0))
    row_mask = jnp.where((token_rows >= first) & (token_rows < first + width), 1.0, 0.0)

    halo[0].wait_recv()
    conv_sum = conv_sum + jnp.where(me > 0, 1.0, 0.0) * conv_terms(0, rows3[0])
    halo[1].wait_recv()
    conv_sum = conv_sum + jnp.where(me < PEERS - 1, 1.0, 0.0) * conv_terms(2, rows3[2])
    inner = (silu(conv_sum) * row_mask).astype(BF16)
    inner_s[...] = inner

    def part_copy(group, k):
        sem = 4 + 3 * group + k - 1
        return pltpu.make_async_remote_copy(
            src_ref=part.at[group], dst_ref=part_in.at[group, k - 1],
            send_sem=ssem.at[sem], recv_sem=rsem.at[sem],
            device_id=(me, lax.rem(team + k, TEAM)), device_id_type=MESH,
        )

    own = []
    for group in range(2):
        own.append(nt(xw[group * GROUP : (group + 1) * GROUP, :], inner))
        part[group] = own[group].astype(BF16)
        for k in (2, 1, 3):
            part_copy(group, k).start()

    def exchange(sem, src, dst, slot_there):
        def one(i, _):
            peer = away(i)
            pltpu.make_async_remote_copy(
                src_ref=src.at[pl.ds(slot_there(me, peer)[0], 1)], dst_ref=dst.at[pl.ds(slot_there(me, peer)[1], 1)],
                send_sem=ssem.at[sem], recv_sem=rsem.at[sem], device_id=(peer, team), device_id_type=MESH,
            ).start()
            return _

        lax.fori_loop(0, PEERS - 1, one, 0)
        here, there = slot_there(me, me)
        own_row = src.at[pl.ds(here, 1)]
        pltpu.make_async_copy(own_row, dst.at[pl.ds(there, 1)], rsem.at[sem]).start()
        pltpu.make_async_copy(own_row, spare.at[pl.ds(sem - 10, 1), pl.ds(0, src.shape[1])], ssem.at[sem]).start()
        due[sem] = all_rows(sem, src, dst)
        sent.append(due[sem])

    def arrive(sem):
        due.pop(sem).wait_recv()

    sent = list(halo)
    due = {}

    def all_rows(sem, src, dst):
        return pltpu.make_async_remote_copy(
            src_ref=src, dst_ref=dst,
            send_sem=ssem.at[sem], recv_sem=rsem.at[sem], device_id=(below, team), device_id_type=MESH,
        )

    plain = lambda src, dst: (dst, src)

    places = [
        one_hot((WIDE, PACK), lambda e, l, b=b: (l == CHAN * b + e) & (e < CHAN)) for b in range(2)
    ]
    pick_cols = [one_hot((PEERS, LEN), lambda j, p, b=b: token_of(p) == 2 * j + b) for b in range(2)]
    put_cols = [one_hot((LEN, PEERS), lambda p, j, b=b: token_of(p) == 2 * j + b) for b in range(2)]
    pick_rows = [one_hot((PEERS, LEN), lambda r, p, b=b: token_of(p) == PEERS * b + r) for b in range(2)]
    put_rows = [one_hot((LEN, PEERS), lambda p, r, b=b: token_of(p) == PEERS * b + r) for b in range(2)]

    def pack(picked):
        return nn(picked[0].astype(BF16), places[0]) + nn(picked[1].astype(BF16), places[1])

    def unpack(message, puts):
        message = message.astype(BF16)
        return nn(puts[0], nt(message, places[0]).astype(BF16)) + nn(puts[1], nt(message, places[1]).astype(BF16))

    send_a[...] = pack([nn(pick_cols[b], inner) for b in range(2)])
    exchange(10, send_a, recv_a, plain)

    def projected(group):
        total = own[group]
        for k in range(1, TEAM):
            part_copy(group, k).wait_recv()
            total = total + part_in[group, k - 1].astype(F32)
        return total.astype(BF16)

    aug[0, 0:GROUP, :] = projected(0)
    place_lane = iota((16, LEN), 1)
    token_lane = token_of(place_lane)
    aug[0, GROUP : GROUP + 16, :] = jnp.where((token_lane >= first) & (token_lane < first + width), 1.0, 0.0).astype(BF16)
    send_b[...] = pack([nt(pick_cols[b], aug[0]) for b in range(2)])
    exchange(11, send_b, recv_b, plain)

    aug[1, 0:GROUP, :] = projected(1)
    identity = one_hot((LEN, LEN), lambda r, c: r == c)
    sub = iota((8, WIDE), 0)

    def prepare(pair, features, inner_b, mask_b):
        proj[pair] = features
        pre = nn(features[:, 0:LEN].astype(BF16), dtw[1 - pair])
        for second in range(2):
            d = 2 * second + pair
            v = pre[:, WIDE * second : WIDE * second + WIDE].astype(BF16).astype(F32) + bias[d : d + 1, :]
            size = mask_b * (jnp.maximum(v, 0.0) + jnp.log1p(jnp.exp(-jnp.abs(v))))
            step[d] = size
            drive[d] = size * inner_b

    def at(q, second):
        p = STEPS - 1 - q if second else q
        return pl.multiple_of(p * 8, 8)

    def gates(pair, second, rows):
        base = 2 * RANK + 2 * STATE * second
        tile = proj[pair, pl.ds(rows, 8), :]
        ins = [jnp.broadcast_to(tile[:, base + n : base + n + 1], (8, WIDE)) for n in range(STATE)]
        outs = [jnp.broadcast_to(tile[:, base + STATE + n : base + STATE + n + 1], (8, WIDE)) for n in range(STATE)]
        return ins, outs

    def roll_on(x, s, second, fill):
        moved = pltpu.roll(x, 8 - s if second else s, 0)
        keep = sub < 8 - s if second else sub >= s
        return jnp.where(keep, moved, fill)

    def totals(pair):
        part_states = STATE // 2
        zero = jnp.zeros((8, WIDE), F32)
        ends = {}
        for base in range(0, STATE, part_states):

            def advance(q, carry):
                new = []
                for second in range(2):
                    d, rows = 2 * second + pair, at(q, second)
                    size, push = step[d, pl.ds(rows, 8), :], drive[d, pl.ds(rows, 8), :]
                    tile = proj[pair, pl.ds(rows, 8), :]
                    lane = 2 * RANK + 2 * STATE * second + base
                    for n in range(part_states):
                        now = jnp.exp2(decay[d, base + n : base + n + 1, :] * size)
                        gate_in = jnp.broadcast_to(tile[:, lane + n : lane + n + 1], (8, WIDE))
                        new.append(now * carry[part_states * second + n] + push * gate_in)
                return tuple(new)

            got = lax.fori_loop(0, STEPS, advance, (zero,) * (2 * part_states), unroll=4)
            for second in range(2):
                for n in range(part_states):
                    ends[second, base + n] = got[part_states * second + n]
        for second in range(2):
            d = 2 * second + pair
            chunk = step[d, 0:8, :]
            for q in range(1, STEPS):
                chunk = chunk + step[d, 8 * q : 8 * q + 8, :]
            run = chunk
            for s in (1, 2, 4):
                run = run + roll_on(run, s, second, 0.0)
            carry_p[d] = roll_on(run, 1, second, 0.0)
            end = 0 if second else 7
            for n in range(STATE):
                h, p = ends[second, n], jnp.exp2(decay[d, n : n + 1, :] * chunk)
                for s in (1, 2, 4):
                    h = p * roll_on(h, s, second, 0.0) + h
                    if s < 4:
                        p = p * roll_on(p, s, second, 1.0)
                hexc[d, 8 * n : 8 * n + 8, :] = roll_on(h, 1, second, 0.0)
                for half in range(2):
                    k = 32 * second + 16 * half + n
                    send_h[pair, k : k + 1, 0:LEN] = h[end : end + 1, LEN * half : LEN * half + LEN]
            whole = jnp.exp2(decay[d] * run[end : end + 1, :])
            for half in range(2):
                k = 32 * second + 16 * half
                send_h[pair, k : k + STATE, LEN : 2 * LEN] = whole[:, LEN * half : LEN * half + LEN]

    def place_in_order(source, owner):
        return jnp.where(owner < PEERS // 2, source, PEERS - 1 - source)

    def send_totals(pair):
        exchange(
            12 + pair, send_h.at[pair], recv_h.at[pair], lambda src, dst: (dst, place_in_order(src, dst))
        )

    def own_scan(pair):
        arrive(12 + pair)
        h, p = recv_h[pair, :, 0:LEN], recv_h[pair, :, LEN : 2 * LEN]
        row = iota((PEERS, LEN), 0)
        for s in (1, 2, 4, 8, 16, 32):
            keep = row >= s
            h = p * jnp.where(keep, pltpu.roll(h, s, 0), 0.0) + h
            if s < 32:
                p = p * jnp.where(keep, pltpu.roll(p, s, 0), 1.0)
        send_c[pair] = jnp.where(row >= 1, pltpu.roll(h, 1, 0), 0.0)
        exchange(
            14 + pair, send_c.at[pair], recv_c.at[pair], lambda src, dst: (place_in_order(dst, src), src)
        )

    def local_pass(pair):
        for second in range(2):
            d = 2 * second + pair

            def advance(q, carry):
                rows = at(q, second)
                size, push = step[d, pl.ds(rows, 8), :], drive[d, pl.ds(rows, 8), :]
                ins, outs = gates(pair, second, rows)
                since = carry[STATE] + size
                new, y = [], jnp.zeros((8, WIDE), F32)
                for n in range(STATE):
                    rate = decay[d, n : n + 1, :]
                    h = jnp.exp2(rate * size) * carry[n] + push * ins[n]
                    y = y + outs[n] * h
                    cc[d, pl.ds(rows * STATE + 8 * n, 8), :] = outs[n] * jnp.exp2(rate * since)
                    new.append(h)
                local[d, pl.ds(rows, 8), :] = y
                return tuple(new) + (since,)

            lax.fori_loop(
                0, STEPS, advance,
                tuple(hexc[d, 8 * n : 8 * n + 8, :] for n in range(STATE)) + (carry_p[d],),
            )

    def finish(pair, dst):
        arrive(14 + pair)

        def advance(p, _):
            rows = pl.multiple_of(p * 8, 8)
            for half in range(2):
                lanes = slice(LEN * half, LEN * half + LEN)
                sums = [local[pair, pl.ds(rows, 8), lanes], local[2 + pair, pl.ds(rows, 8), lanes], None, None]
                for n in range(STATE):
                    for second in range(2):
                        k = 32 * second + 16 * half + n
                        term = cc[2 * second + pair, pl.ds(rows * STATE + 8 * n, 8), lanes] * recv_c[pair, k : k + 1, :]
                        spot = (2 * n + second) % 4
                        sums[spot] = term if sums[spot] is None else sums[spot] + term
                dst[pl.ds(rows, 8), lanes] = (sums[0] + sums[1]) + (sums[2] + sums[3])
            return _

        lax.fori_loop(0, STEPS, advance, 0, unroll=4)

    inner_f = inner.astype(F32)
    prepare(0, nt(identity, aug[1]), inner_f, row_mask)
    totals(0)
    send_totals(0)

    arrive(10)
    col_inner = unpack(recv_a[...], put_rows)
    arrive(11)
    col_feat = unpack(recv_b[...], put_rows)
    prepare(1, col_feat, col_inner, jnp.broadcast_to(col_feat[:, GROUP : GROUP + 1], (LEN, WIDE)))
    totals(1)
    send_totals(1)
    own_scan(0)
    local_pass(1)
    own_scan(1)
    local_pass(0)
    finish(1, ycol)
    back = ycol[...].astype(BF16)
    send_y[...] = pack([nn(pick_rows[b], back) for b in range(2)])
    exchange(16, send_y, recv_y, plain)
    finish(0, yrow)
    natural = one_hot((LEN, LEN), lambda p, t: token_of(p) == t)
    base = yrow[...] + skips[0:1, :] * inner_s[...].astype(F32)
    high = base.astype(BF16)
    base = (tn(high, natural) + tn((base - high.astype(F32)).astype(BF16), natural))[0:CHAN]
    gated = silu(gate[...].astype(F32))
    arrive(16)
    back = recv_y[...].astype(BF16)
    spots = [one_hot((PEERS, LEN), lambda j, t, b=b: t == 2 * j + b) for b in range(2)]
    returned = tn(back, spots[0])[0:CHAN] + tn(back, spots[1])[CHAN:PACK]
    out[...] = ((base + returned) * gated).astype(BF16)

    for copy in sent:
        copy.wait_send()
    for group in range(2):
        for k in range(1, TEAM):
            part_copy(group, k).wait_send()


def body(
    feats, gate_in, conv_weight, conv_bias, xproj_weight, dtproj_weight, dt_bias, a_log, skip_gain, row_start, row_len
):
    vmem = pl.BlockSpec(memory_space=pltpu.VMEM)
    hbm = pl.BlockSpec(memory_space=pltpu.HBM)
    inputs = [
        ((CHAN, LEN), BF16), ((CHAN, LEN), BF16), ((9, CHAN), F32), ((1, CHAN), F32), ((CHAN, 2 * GROUP), BF16),
        ((4, RANK, CHAN), BF16), ((4, CHAN), F32), ((4, STATE, CHAN), F32), ((4, CHAN), F32),
    ]
    scratch = [
        ((3, WIDE, LEN), BF16),
        ((16, WIDE), F32),
        ((2 * GROUP, WIDE), BF16),
        ((2, GROUP, LEN), BF16),
        ((2, TEAM - 1, GROUP, LEN), BF16),
        ((2, LEN, 2 * WIDE), BF16),
        ((8, WIDE), F32),
        ((4, STATE, WIDE), F32),
        ((8, WIDE), F32),
        ((2, WIDE, LEN), BF16),
        ((4, LEN, WIDE), F32),
        ((4, LEN, WIDE), F32),
        ((2, LEN, WIDE), F32),
        ((4, STATE * 8, WIDE), F32),
        ((4, LEN, WIDE), F32),
        ((4, LEN * STATE, WIDE), F32),
        ((4, 8, WIDE), F32),
        ((PEERS, PACK), F32), ((PEERS, PACK), F32),
        ((PEERS, PACK), F32), ((PEERS, PACK), F32),
        ((2, PEERS, WIDE), F32), ((2, PEERS, WIDE), F32),
        ((2, PEERS, LEN), F32), ((2, PEERS, LEN), F32),
        ((PEERS, PACK), F32), ((PEERS, PACK), F32),
        ((LEN, WIDE), BF16),
        ((LEN, WIDE), F32), ((LEN, WIDE), F32),
        ((8, PACK), F32),
    ]
    return pl.pallas_call(
        body_kernel,
        out_shape=jax.ShapeDtypeStruct((CHAN, LEN), BF16),
        in_specs=[hbm] * 11,
        out_specs=vmem,
        scratch_shapes=[pltpu.VMEM(s, t) for s, t in inputs] + [pltpu.SMEM((1, 1), jnp.int32)] * 2
        + [pltpu.VMEM(s, t) for s, t in scratch]
        + [pltpu.SemaphoreType.DMA((17,)), pltpu.SemaphoreType.DMA((17,)), pltpu.SemaphoreType.DMA((11,))],
        compiler_params=pltpu.CompilerParams(
            collective_id=0, has_side_effects=True, vmem_limit_bytes=56 * 1024 * 1024
        ),
    )(
        feats, gate_in, conv_weight, conv_bias.reshape(1, CHAN), xproj_weight, dtproj_weight, dt_bias,
        jnp.swapaxes(a_log, 1, 2), skip_gain, row_start.reshape(1, 1), row_len.reshape(1, 1),
    )


def solution(mesh):
    in_specs = (
        P("chan", "tissue"),
        P("chan", "tissue"),
        P(None, "chan"),
        P("chan"),
        P("chan", None),
        P(None, None, "chan"),
        P(None, "chan"),
        P(None, "chan", None),
        P(None, "chan"),
        P("tissue"),
        P("tissue"),
    )
    return jax.shard_map(body, mesh=mesh, in_specs=in_specs, out_specs=P("chan", "tissue"), check_vma=False)
```

```python
import jax
import jax.numpy as jnp
from jax import lax
from jax.experimental import pallas as pl
from jax.experimental.pallas import tpu as pltpu
from jax.sharding import PartitionSpec as P

MESH = pl.DeviceIdType.MESH
F32 = jnp.float32
BF16 = jnp.bfloat16
PEERS = 64
TEAM = 4
LEN = 128
CHAN = 192
WIDE = 256
STATE = 16
RANK = 48
GROUP = 2 * (RANK + 2 * STATE)
PACK = 2 * CHAN
STEPS = 16
LOG2E = 1.4426950408889634


def nn(a, b):
    return lax.dot_general(a, b, (((1,), (0,)), ((), ())), preferred_element_type=F32)


def nt(a, b):
    return lax.dot_general(a, b, (((1,), (1,)), ((), ())), preferred_element_type=F32)


def tn(a, b):
    return lax.dot_general(a, b, (((0,), (0,)), ((), ())), preferred_element_type=F32)


def token_of(place):
    return (place & 7) * STEPS + (place >> 3)


def iota(shape, dim):
    return lax.broadcasted_iota(jnp.int32, shape, dim)


def one_hot(shape, equal):
    return jnp.where(equal(iota(shape, 0), iota(shape, 1)), 1.0, 0.0).astype(BF16)


def silu(v):
    return v / (1.0 + jnp.exp(-v))


def body_kernel(
    feats_hbm, gate_hbm, conv_w_hbm, conv_b_hbm, xproj_hbm, dtproj_hbm, dt_bias_hbm, a_log_hbm, skip_hbm, start_hbm, len_hbm,
    out,
    feats, gate, conv_w, conv_b, xproj, dtproj, dt_bias, a_log, skip, row_start, row_len,
    rows3, convp, xw, part, part_in, dtw, bias, decay, skips, aug,
    step, drive, proj, hexc, local, cc, carry_p,
    send_a, recv_a, send_b, recv_b, send_h, recv_h, send_c, recv_c, send_y, recv_y,
    inner_s, yrow, ycol, spare,
    ssem, rsem, isem,
):
    me = lax.axis_index("tissue")
    team = lax.axis_index("chan")

    barrier = pltpu.get_barrier_semaphore()

    plane, core = me >> 4, me & 1
    lines = [(((me >> 1) + dz) & 7) * 2 for dz in (4, 3, 5, 2, 6, 1, 7, 0)]

    def to_peers(act):
        def one(q, _):
            base = ((plane + 2 + (q >> 1) - (q & 1)) & 3) * 16
            for line in lines:
                for other in (1 - core, core):
                    act(base + line + other)
            return _

        lax.fori_loop(0, 3, one, 0)
        for line in lines:
            act(plane * 16 + line + 1 - core)
        for line in lines[:-1]:
            act(plane * 16 + line + core)

    to_peers(lambda peer: pl.semaphore_signal(barrier, inc=1, device_id=(peer, team), device_id_type=MESH))
    for k in (2, 1, 3):
        pl.semaphore_signal(barrier, inc=1, device_id=(me, lax.rem(team + k, TEAM)), device_id_type=MESH)

    loads = [
        pltpu.make_async_copy(src, dst, isem.at[n])
        for n, (src, dst) in enumerate((
            (start_hbm, row_start), (len_hbm, row_len), (feats_hbm, feats), (xproj_hbm, xproj), (conv_w_hbm, conv_w),
            (conv_b_hbm, conv_b), (dtproj_hbm, dtproj), (dt_bias_hbm, dt_bias), (a_log_hbm, a_log), (skip_hbm, skip),
            (gate_hbm, gate),
        ))
    ]
    for load in loads:
        load.start()
    rows3[:, CHAN:, :] = jnp.zeros((3, WIDE - CHAN, LEN), BF16)
    for load in loads:
        load.wait()

    first, width = row_start[0, 0], row_len[0, 0]
    cols = iota((CHAN, LEN), 1)
    lane_mask = (cols >= first) & (cols < first + width)
    rows3[1, 0:CHAN, :] = jnp.where(lane_mask, feats[...], jnp.zeros((), BF16))

    shifts = one_hot((3 * LEN, LEN), lambda r, t: t == token_of(r & (LEN - 1)) + (r >> 7) - 1)
    convp[...] = jnp.zeros_like(convp)
    convp[0:9, 0:CHAN] = conv_w[...]
    convp[9:10, 0:CHAN] = conv_b[...]
    bias[...] = jnp.zeros_like(bias)
    bias[0:4, 0:CHAN] = dt_bias[...]
    skips[...] = jnp.zeros_like(skips)
    skips[0:1, 0:CHAN] = jnp.sum(skip[...], axis=0, keepdims=True)
    aug[...] = jnp.zeros_like(aug)

    turned = nt(one_hot((2 * GROUP, 2 * GROUP), lambda r, f: r == f), xproj[...]).astype(BF16)
    xw[...] = jnp.zeros_like(xw)
    for d in range(4):
        top, start = GROUP * (1 - d % 2), (RANK + 2 * STATE) * d
        low, gat = top + RANK * (d // 2), top + 2 * RANK + 2 * STATE * (d // 2)
        xw[low : low + RANK, 0:CHAN] = turned[start : start + RANK]
        xw[gat : gat + 2 * STATE, 0:CHAN] = turned[start + RANK : start + RANK + 2 * STATE]

    dtw[...] = jnp.zeros_like(dtw)
    for d in range(4):
        pair, second = 1 - d % 2, d // 2
        dtw[pair, RANK * second : RANK * second + RANK, WIDE * second : WIDE * second + CHAN] = dtproj[d]
    decay[...] = jnp.zeros_like(decay)
    for d in range(4):
        decay[d, :, 0:CHAN] = -LOG2E * jnp.exp(a_log[d])

    pl.semaphore_wait(barrier, PEERS - 1 + TEAM - 1)

    below = lax.rem(me + 1, PEERS)
    above = lax.rem(me + PEERS - 1, PEERS)
    halo = [
        pltpu.make_async_remote_copy(
            src_ref=rows3.at[1, pl.ds(0, CHAN)], dst_ref=rows3.at[slot, pl.ds(0, CHAN)],
            send_sem=ssem.at[slot], recv_sem=rsem.at[slot], device_id=(peer, team), device_id_type=MESH,
        )
        for slot, peer in ((0, below), (2, above))
    ]
    for copy in halo:
        copy.start()

    def conv_terms(i, source):
        x = nt(shifts, source)
        total = None
        for j in range(3):
            term = convp[3 * i + j : 3 * i + j + 1, :] * x[j * LEN : (j + 1) * LEN]
            total = term if total is None else total + term
        return total

    conv_sum = convp[9:10, :] + conv_terms(1, rows3[1])
    token_rows = token_of(iota((LEN, WIDE), 0))
    row_mask = jnp.where((token_rows >= first) & (token_rows < first + width), 1.0, 0.0)

    halo[0].wait_recv()
    conv_sum = conv_sum + jnp.where(me > 0, 1.0, 0.0) * conv_terms(0, rows3[0])
    halo[1].wait_recv()
    conv_sum = conv_sum + jnp.where(me < PEERS - 1, 1.0, 0.0) * conv_terms(2, rows3[2])
    inner = (silu(conv_sum) * row_mask).astype(BF16)
    inner_s[...] = inner

    def part_copy(group, k):
        sem = 4 + 3 * group + k - 1
        return pltpu.make_async_remote_copy(
            src_ref=part.at[group], dst_ref=part_in.at[group, k - 1],
            send_sem=ssem.at[sem], recv_sem=rsem.at[sem],
            device_id=(me, lax.rem(team + k, TEAM)), device_id_type=MESH,
        )

    own = []
    for group in range(2):
        own.append(nt(xw[group * GROUP : (group + 1) * GROUP, :], inner))
        part[group] = own[group].astype(BF16)
        for k in (2, 1, 3):
            part_copy(group, k).start()

    def exchange(sem, src, dst, slot_there):
        def send(peer):
            here, there = slot_there(me, peer)
            pltpu.make_async_remote_copy(
                src_ref=src.at[pl.ds(here, 1)], dst_ref=dst.at[pl.ds(there, 1)],
                send_sem=ssem.at[sem], recv_sem=rsem.at[sem], device_id=(peer, team), device_id_type=MESH,
            ).start()

        to_peers(send)
        here, there = slot_there(me, me)
        own_row = src.at[pl.ds(here, 1)]
        pltpu.make_async_copy(own_row, dst.at[pl.ds(there, 1)], rsem.at[sem]).start()
        pltpu.make_async_copy(own_row, spare.at[pl.ds(sem - 10, 1), pl.ds(0, src.shape[1])], ssem.at[sem]).start()
        due[sem] = all_rows(sem, src, dst)
        sent.append(due[sem])

    def arrive(sem):
        due.pop(sem).wait_recv()

    sent = list(halo)
    due = {}

    def all_rows(sem, src, dst):
        return pltpu.make_async_remote_copy(
            src_ref=src, dst_ref=dst,
            send_sem=ssem.at[sem], recv_sem=rsem.at[sem], device_id=(below, team), device_id_type=MESH,
        )

    plain = lambda src, dst: (dst, src)

    places = [
        one_hot((WIDE, PACK), lambda e, l, b=b: (l == CHAN * b + e) & (e < CHAN)) for b in range(2)
    ]
    pick_cols = [one_hot((PEERS, LEN), lambda j, p, b=b: token_of(p) == 2 * j + b) for b in range(2)]
    put_cols = [one_hot((LEN, PEERS), lambda p, j, b=b: token_of(p) == 2 * j + b) for b in range(2)]
    pick_rows = [one_hot((PEERS, LEN), lambda r, p, b=b: token_of(p) == PEERS * b + r) for b in range(2)]
    put_rows = [one_hot((LEN, PEERS), lambda p, r, b=b: token_of(p) == PEERS * b + r) for b in range(2)]

    def pack(picked):
        return nn(picked[0].astype(BF16), places[0]) + nn(picked[1].astype(BF16), places[1])

    def unpack(message, puts):
        message = message.astype(BF16)
        return nn(puts[0], nt(message, places[0]).astype(BF16)) + nn(puts[1], nt(message, places[1]).astype(BF16))

    send_a[...] = pack([nn(pick_cols[b], inner) for b in range(2)])
    exchange(10, send_a, recv_a, plain)

    def projected(group):
        total = own[group]
        for k in range(1, TEAM):
            part_copy(group, k).wait_recv()
            total = total + part_in[group, k - 1].astype(F32)
        return total.astype(BF16)

    aug[0, 0:GROUP, :] = projected(0)
    place_lane = iota((16, LEN), 1)
    token_lane = token_of(place_lane)
    aug[0, GROUP : GROUP + 16, :] = jnp.where((token_lane >= first) & (token_lane < first + width), 1.0, 0.0).astype(BF16)
    send_b[...] = pack([nt(pick_cols[b], aug[0]) for b in range(2)])
    exchange(11, send_b, recv_b, plain)

    aug[1, 0:GROUP, :] = projected(1)
    identity = one_hot((LEN, LEN), lambda r, c: r == c)
    sub = iota((8, WIDE), 0)

    def prepare(pair, features, inner_b, mask_b):
        proj[pair] = features
        pre = nn(features[:, 0:LEN].astype(BF16), dtw[1 - pair])
        for second in range(2):
            d = 2 * second + pair
            v = pre[:, WIDE * second : WIDE * second + WIDE].astype(BF16).astype(F32) + bias[d : d + 1, :]
            size = mask_b * (jnp.maximum(v, 0.0) + jnp.log1p(jnp.exp(-jnp.abs(v))))
            step[d] = size
            drive[d] = size * inner_b

    def at(q, second):
        p = STEPS - 1 - q if second else q
        return pl.multiple_of(p * 8, 8)

    def gates(pair, second, rows):
        base = 2 * RANK + 2 * STATE * second
        tile = proj[pair, pl.ds(rows, 8), :]
        ins = [jnp.broadcast_to(tile[:, base + n : base + n + 1], (8, WIDE)) for n in range(STATE)]
        outs = [jnp.broadcast_to(tile[:, base + STATE + n : base + STATE + n + 1], (8, WIDE)) for n in range(STATE)]
        return ins, outs

    def roll_on(x, s, second, fill):
        moved = pltpu.roll(x, 8 - s if second else s, 0)
        keep = sub < 8 - s if second else sub >= s
        return jnp.where(keep, moved, fill)

    def totals(pair):
        part_states = STATE // 2
        zero = jnp.zeros((8, WIDE), F32)
        ends = {}
        for base in range(0, STATE, part_states):

            def advance(q, carry):
                new = []
                for second in range(2):
                    d, rows = 2 * second + pair, at(q, second)
                    size, push = step[d, pl.ds(rows, 8), :], drive[d, pl.ds(rows, 8), :]
                    tile = proj[pair, pl.ds(rows, 8), :]
                    lane = 2 * RANK + 2 * STATE * second + base
                    for n in range(part_states):
                        now = jnp.exp2(decay[d, base + n : base + n + 1, :] * size)
                        gate_in = jnp.broadcast_to(tile[:, lane + n : lane + n + 1], (8, WIDE))
                        new.append(now * carry[part_states * second + n] + push * gate_in)
                return tuple(new)

            got = lax.fori_loop(0, STEPS, advance, (zero,) * (2 * part_states), unroll=4)
            for second in range(2):
                for n in range(part_states):
                    ends[second, base + n] = got[part_states * second + n]
        for second in range(2):
            d = 2 * second + pair
            chunk = step[d, 0:8, :]
            for q in range(1, STEPS):
                chunk = chunk + step[d, 8 * q : 8 * q + 8, :]
            run = chunk
            for s in (1, 2, 4):
                run = run + roll_on(run, s, second, 0.0)
            carry_p[d] = roll_on(run, 1, second, 0.0)
            end = 0 if second else 7
            for n in range(STATE):
                h, p = ends[second, n], jnp.exp2(decay[d, n : n + 1, :] * chunk)
                for s in (1, 2, 4):
                    h = p * roll_on(h, s, second, 0.0) + h
                    if s < 4:
                        p = p * roll_on(p, s, second, 1.0)
                hexc[d, 8 * n : 8 * n + 8, :] = roll_on(h, 1, second, 0.0)
                for half in range(2):
                    k = 32 * second + 16 * half + n
                    send_h[pair, k : k + 1, 0:LEN] = h[end : end + 1, LEN * half : LEN * half + LEN]
            whole = jnp.exp2(decay[d] * run[end : end + 1, :])
            for half in range(2):
                k = 32 * second + 16 * half
                send_h[pair, k : k + STATE, LEN : 2 * LEN] = whole[:, LEN * half : LEN * half + LEN]

    def place_in_order(source, owner):
        return jnp.where(owner < PEERS // 2, source, PEERS - 1 - source)

    def send_totals(pair):
        exchange(
            12 + pair, send_h.at[pair], recv_h.at[pair], lambda src, dst: (dst, place_in_order(src, dst))
        )

    def own_scan(pair):
        arrive(12 + pair)
        h, p = recv_h[pair, :, 0:LEN], recv_h[pair, :, LEN : 2 * LEN]
        row = iota((PEERS, LEN), 0)
        for s in (1, 2, 4, 8, 16, 32):
            keep = row >= s
            h = p * jnp.where(keep, pltpu.roll(h, s, 0), 0.0) + h
            if s < 32:
                p = p * jnp.where(keep, pltpu.roll(p, s, 0), 1.0)
        send_c[pair] = jnp.where(row >= 1, pltpu.roll(h, 1, 0), 0.0)
        exchange(
            14 + pair, send_c.at[pair], recv_c.at[pair], lambda src, dst: (place_in_order(dst, src), src)
        )

    def local_pass(pair):
        for second in range(2):
            d = 2 * second + pair

            def advance(q, carry):
                rows = at(q, second)
                size, push = step[d, pl.ds(rows, 8), :], drive[d, pl.ds(rows, 8), :]
                ins, outs = gates(pair, second, rows)
                since = carry[STATE] + size
                new, y = [], jnp.zeros((8, WIDE), F32)
                for n in range(STATE):
                    rate = decay[d, n : n + 1, :]
                    h = jnp.exp2(rate * size) * carry[n] + push * ins[n]
                    y = y + outs[n] * h
                    cc[d, pl.ds(rows * STATE + 8 * n, 8), :] = outs[n] * jnp.exp2(rate * since)
                    new.append(h)
                local[d, pl.ds(rows, 8), :] = y
                return tuple(new) + (since,)

            lax.fori_loop(
                0, STEPS, advance,
                tuple(hexc[d, 8 * n : 8 * n + 8, :] for n in range(STATE)) + (carry_p[d],),
            )

    def finish(pair, dst):
        arrive(14 + pair)

        def advance(p, _):
            rows = pl.multiple_of(p * 8, 8)
            for half in range(2):
                lanes = slice(LEN * half, LEN * half + LEN)
                sums = [local[pair, pl.ds(rows, 8), lanes], local[2 + pair, pl.ds(rows, 8), lanes], None, None]
                for n in range(STATE):
                    for second in range(2):
                        k = 32 * second + 16 * half + n
                        term = cc[2 * second + pair, pl.ds(rows * STATE + 8 * n, 8), lanes] * recv_c[pair, k : k + 1, :]
                        spot = (2 * n + second) % 4
                        sums[spot] = term if sums[spot] is None else sums[spot] + term
                dst[pl.ds(rows, 8), lanes] = (sums[0] + sums[1]) + (sums[2] + sums[3])
            return _

        lax.fori_loop(0, STEPS, advance, 0, unroll=4)

    inner_f = inner.astype(F32)
    prepare(0, nt(identity, aug[1]), inner_f, row_mask)
    totals(0)
    send_totals(0)

    arrive(10)
    col_inner = unpack(recv_a[...], put_rows)
    arrive(11)
    col_feat = unpack(recv_b[...], put_rows)
    prepare(1, col_feat, col_inner, jnp.broadcast_to(col_feat[:, GROUP : GROUP + 1], (LEN, WIDE)))
    totals(1)
    send_totals(1)
    local_pass(1)
    own_scan(1)
    own_scan(0)
    local_pass(0)
    finish(1, ycol)
    back = ycol[...].astype(BF16)
    send_y[...] = pack([nn(pick_rows[b], back) for b in range(2)])
    exchange(16, send_y, recv_y, plain)
    finish(0, yrow)
    natural = one_hot((LEN, LEN), lambda p, t: token_of(p) == t)
    base = yrow[...] + skips[0:1, :] * inner_s[...].astype(F32)
    high = base.astype(BF16)
    base = (tn(high, natural) + tn((base - high.astype(F32)).astype(BF16), natural))[0:CHAN]
    gated = silu(gate[...].astype(F32))
    arrive(16)
    back = recv_y[...].astype(BF16)
    spots = [one_hot((PEERS, LEN), lambda j, t, b=b: t == 2 * j + b) for b in range(2)]
    returned = tn(back, spots[0])[0:CHAN] + tn(back, spots[1])[CHAN:PACK]
    out[...] = ((base + returned) * gated).astype(BF16)

    for copy in sent:
        copy.wait_send()
    for group in range(2):
        for k in range(1, TEAM):
            part_copy(group, k).wait_send()


def body(
    feats, gate_in, conv_weight, conv_bias, xproj_weight, dtproj_weight, dt_bias, a_log, skip_gain, row_start, row_len
):
    vmem = pl.BlockSpec(memory_space=pltpu.VMEM)
    hbm = pl.BlockSpec(memory_space=pltpu.HBM)
    inputs = [
        ((CHAN, LEN), BF16), ((CHAN, LEN), BF16), ((9, CHAN), F32), ((1, CHAN), F32), ((CHAN, 2 * GROUP), BF16),
        ((4, RANK, CHAN), BF16), ((4, CHAN), F32), ((4, STATE, CHAN), F32), ((4, CHAN), F32),
    ]
    scratch = [
        ((3, WIDE, LEN), BF16),
        ((16, WIDE), F32),
        ((2 * GROUP, WIDE), BF16),
        ((2, GROUP, LEN), BF16),
        ((2, TEAM - 1, GROUP, LEN), BF16),
        ((2, LEN, 2 * WIDE), BF16),
        ((8, WIDE), F32),
        ((4, STATE, WIDE), F32),
        ((8, WIDE), F32),
        ((2, WIDE, LEN), BF16),
        ((4, LEN, WIDE), F32),
        ((4, LEN, WIDE), F32),
        ((2, LEN, WIDE), F32),
        ((4, STATE * 8, WIDE), F32),
        ((4, LEN, WIDE), F32),
        ((4, LEN * STATE, WIDE), F32),
        ((4, 8, WIDE), F32),
        ((PEERS, PACK), F32), ((PEERS, PACK), F32),
        ((PEERS, PACK), F32), ((PEERS, PACK), F32),
        ((2, PEERS, WIDE), F32), ((2, PEERS, WIDE), F32),
        ((2, PEERS, LEN), F32), ((2, PEERS, LEN), F32),
        ((PEERS, PACK), F32), ((PEERS, PACK), F32),
        ((LEN, WIDE), BF16),
        ((LEN, WIDE), F32), ((LEN, WIDE), F32),
        ((8, PACK), F32),
    ]
    return pl.pallas_call(
        body_kernel,
        out_shape=jax.ShapeDtypeStruct((CHAN, LEN), BF16),
        in_specs=[hbm] * 11,
        out_specs=vmem,
        scratch_shapes=[pltpu.VMEM(s, t) for s, t in inputs] + [pltpu.SMEM((1, 1), jnp.int32)] * 2
        + [pltpu.VMEM(s, t) for s, t in scratch]
        + [pltpu.SemaphoreType.DMA((17,)), pltpu.SemaphoreType.DMA((17,)), pltpu.SemaphoreType.DMA((11,))],
        compiler_params=pltpu.CompilerParams(
            collective_id=0, has_side_effects=True, vmem_limit_bytes=56 * 1024 * 1024
        ),
    )(
        feats, gate_in, conv_weight, conv_bias.reshape(1, CHAN), xproj_weight, dtproj_weight, dt_bias,
        jnp.swapaxes(a_log, 1, 2), skip_gain, row_start.reshape(1, 1), row_len.reshape(1, 1),
    )


def solution(mesh):
    in_specs = (
        P("chan", "tissue"),
        P("chan", "tissue"),
        P(None, "chan"),
        P("chan"),
        P("chan", None),
        P(None, None, "chan"),
        P(None, "chan"),
        P(None, "chan", None),
        P(None, "chan"),
        P("tissue"),
        P("tissue"),
    )
    return jax.shard_map(body, mesh=mesh, in_specs=in_specs, out_specs=P("chan", "tissue"), check_vma=False)
```

```python
import jax
import jax.numpy as jnp
from jax import lax
from jax.experimental import pallas as pl
from jax.experimental.pallas import tpu as pltpu
from jax.sharding import PartitionSpec as P

MESH = pl.DeviceIdType.MESH
F32 = jnp.float32
BF16 = jnp.bfloat16
PEERS = 64
TEAM = 4
LEN = 128
CHAN = 192
WIDE = 256
STATE = 16
RANK = 48
GROUP = 2 * (RANK + 2 * STATE)
PACK = 2 * CHAN
STEPS = 16
LOG2E = 1.4426950408889634


def nn(a, b):
    return lax.dot_general(a, b, (((1,), (0,)), ((), ())), preferred_element_type=F32)


def nt(a, b):
    return lax.dot_general(a, b, (((1,), (1,)), ((), ())), preferred_element_type=F32)


def tn(a, b):
    return lax.dot_general(a, b, (((0,), (0,)), ((), ())), preferred_element_type=F32)


def token_of(place):
    return (place & 7) * STEPS + (place >> 3)


def iota(shape, dim):
    return lax.broadcasted_iota(jnp.int32, shape, dim)


def one_hot(shape, equal):
    return jnp.where(equal(iota(shape, 0), iota(shape, 1)), 1.0, 0.0).astype(BF16)


def silu(v):
    return v / (1.0 + jnp.exp(-v))


def body_kernel(
    feats_hbm, gate_hbm, conv_w_hbm, conv_b_hbm, xproj_hbm, dtproj_hbm, dt_bias_hbm, a_log_hbm, skip_hbm, start_hbm, len_hbm,
    out,
    feats, gate, conv_w, conv_b, xproj, dtproj, dt_bias, a_log, skip, row_start, row_len,
    rows3, convp, xw, part, part_in, dtw, bias, decay, skips, aug,
    step, drive, proj, hexc, local, cc, carry_p,
    send_a, recv_a, send_b, recv_b, send_h, recv_h, send_c, recv_c, send_y, recv_y,
    inner_s, yrow, ycol, spare,
    ssem, rsem, isem,
):
    me = lax.axis_index("tissue")
    team = lax.axis_index("chan")

    barrier = pltpu.get_barrier_semaphore()

    plane, core = me >> 4, me & 1
    lines = [(((me >> 1) + dz) & 7) * 2 for dz in (4, 3, 5, 2, 6, 1, 7, 0)]

    def to_peers(act):
        def one(q, _):
            base = ((plane + 2 + (q >> 1) - (q & 1)) & 3) * 16
            for line in lines:
                for other in (1 - core, core):
                    act(base + line + other)
            return _

        lax.fori_loop(0, 3, one, 0)
        for line in lines:
            act(plane * 16 + line + 1 - core)
        for line in lines[:-1]:
            act(plane * 16 + line + core)

    to_peers(lambda peer: pl.semaphore_signal(barrier, inc=1, device_id=(peer, team), device_id_type=MESH))
    for k in (2, 1, 3):
        pl.semaphore_signal(barrier, inc=1, device_id=(me, lax.rem(team + k, TEAM)), device_id_type=MESH)

    loads = [
        pltpu.make_async_copy(src, dst, isem.at[n])
        for n, (src, dst) in enumerate((
            (start_hbm, row_start), (len_hbm, row_len), (feats_hbm, feats), (xproj_hbm, xproj), (conv_w_hbm, conv_w),
            (conv_b_hbm, conv_b), (dtproj_hbm, dtproj), (dt_bias_hbm, dt_bias), (a_log_hbm, a_log), (skip_hbm, skip),
            (gate_hbm, gate),
        ))
    ]
    for load in loads:
        load.start()
    rows3[:, CHAN:, :] = jnp.zeros((3, WIDE - CHAN, LEN), BF16)
    for load in loads:
        load.wait()

    first, width = row_start[0, 0], row_len[0, 0]
    cols = iota((CHAN, LEN), 1)
    lane_mask = (cols >= first) & (cols < first + width)
    rows3[1, 0:CHAN, :] = jnp.where(lane_mask, feats[...], jnp.zeros((), BF16))

    shifts = one_hot((3 * LEN, LEN), lambda r, t: t == token_of(r & (LEN - 1)) + (r >> 7) - 1)
    convp[...] = jnp.zeros_like(convp)
    convp[0:9, 0:CHAN] = conv_w[...]
    convp[9:10, 0:CHAN] = conv_b[...]
    bias[...] = jnp.zeros_like(bias)
    bias[0:4, 0:CHAN] = dt_bias[...]
    skips[...] = jnp.zeros_like(skips)
    skips[0:1, 0:CHAN] = jnp.sum(skip[...], axis=0, keepdims=True)
    aug[...] = jnp.zeros_like(aug)

    turned = nt(one_hot((2 * GROUP, 2 * GROUP), lambda r, f: r == f), xproj[...]).astype(BF16)
    xw[...] = jnp.zeros_like(xw)
    for d in range(4):
        top, start = GROUP * (1 - d % 2), (RANK + 2 * STATE) * d
        low, gat = top + RANK * (d // 2), top + 2 * RANK + 2 * STATE * (d // 2)
        xw[low : low + RANK, 0:CHAN] = turned[start : start + RANK]
        xw[gat : gat + 2 * STATE, 0:CHAN] = turned[start + RANK : start + RANK + 2 * STATE]

    dtw[...] = jnp.zeros_like(dtw)
    for d in range(4):
        pair, second = 1 - d % 2, d // 2
        dtw[pair, RANK * second : RANK * second + RANK, WIDE * second : WIDE * second + CHAN] = dtproj[d]
    decay[...] = jnp.zeros_like(decay)
    for d in range(4):
        decay[d, :, 0:CHAN] = -LOG2E * jnp.exp(a_log[d])

    pl.semaphore_wait(barrier, PEERS - 1 + TEAM - 1)

    below = lax.rem(me + 1, PEERS)
    above = lax.rem(me + PEERS - 1, PEERS)
    halo = [
        pltpu.make_async_remote_copy(
            src_ref=rows3.at[1, pl.ds(0, CHAN)], dst_ref=rows3.at[slot, pl.ds(0, CHAN)],
            send_sem=ssem.at[slot], recv_sem=rsem.at[slot], device_id=(peer, team), device_id_type=MESH,
        )
        for slot, peer in ((0, below), (2, above))
    ]
    for copy in halo:
        copy.start()

    def conv_terms(i, source):
        x = nt(shifts, source)
        total = None
        for j in range(3):
            term = convp[3 * i + j : 3 * i + j + 1, :] * x[j * LEN : (j + 1) * LEN]
            total = term if total is None else total + term
        return total

    conv_sum = convp[9:10, :] + conv_terms(1, rows3[1])
    token_rows = token_of(iota((LEN, WIDE), 0))
    row_mask = jnp.where((token_rows >= first) & (token_rows < first + width), 1.0, 0.0)

    halo[0].wait_recv()
    conv_sum = conv_sum + jnp.where(me > 0, 1.0, 0.0) * conv_terms(0, rows3[0])
    halo[1].wait_recv()
    conv_sum = conv_sum + jnp.where(me < PEERS - 1, 1.0, 0.0) * conv_terms(2, rows3[2])
    inner = (silu(conv_sum) * row_mask).astype(BF16)
    inner_s[...] = inner

    def part_copy(group, k):
        sem = 4 + 3 * group + k - 1
        return pltpu.make_async_remote_copy(
            src_ref=part.at[group], dst_ref=part_in.at[group, k - 1],
            send_sem=ssem.at[sem], recv_sem=rsem.at[sem],
            device_id=(me, lax.rem(team + k, TEAM)), device_id_type=MESH,
        )

    own = []
    for group in range(2):
        own.append(nt(xw[group * GROUP : (group + 1) * GROUP, :], inner))
        part[group] = own[group].astype(BF16)
        for k in (2, 1, 3):
            part_copy(group, k).start()

    def exchange(sem, src, dst, slot_there):
        def send(peer):
            here, there = slot_there(me, peer)
            pltpu.make_async_remote_copy(
                src_ref=src.at[pl.ds(here, 1)], dst_ref=dst.at[pl.ds(there, 1)],
                send_sem=ssem.at[sem], recv_sem=rsem.at[sem], device_id=(peer, team), device_id_type=MESH,
            ).start()

        to_peers(send)
        here, there = slot_there(me, me)
        own_row = src.at[pl.ds(here, 1)]
        pltpu.make_async_copy(own_row, dst.at[pl.ds(there, 1)], rsem.at[sem]).start()
        pltpu.make_async_copy(own_row, spare.at[pl.ds(sem - 10, 1), pl.ds(0, src.shape[1])], ssem.at[sem]).start()
        due[sem] = all_rows(sem, src, dst)
        sent.append(due[sem])

    def arrive(sem):
        due.pop(sem).wait_recv()

    sent = list(halo)
    due = {}

    def all_rows(sem, src, dst):
        return pltpu.make_async_remote_copy(
            src_ref=src, dst_ref=dst,
            send_sem=ssem.at[sem], recv_sem=rsem.at[sem], device_id=(below, team), device_id_type=MESH,
        )

    plain = lambda src, dst: (dst, src)

    places = one_hot(
        (2 * WIDE, PACK), lambda e, l: (l == CHAN * (e >> 8) + (e & (WIDE - 1))) & ((e & (WIDE - 1)) < CHAN)
    )
    pick_cols = one_hot((LEN, LEN), lambda m, p: token_of(p) == 2 * (m & (PEERS - 1)) + (m >> 6))
    pick_rows = one_hot((LEN, LEN), lambda m, p: token_of(p) == m)
    put_rows = one_hot((LEN, LEN), lambda p, m: token_of(p) == m)

    def pack(picked):
        picked = picked.astype(BF16)
        return nn(picked[0:PEERS], places[0:WIDE]) + nn(picked[PEERS:], places[WIDE:])

    def unpack(message, puts):
        apart = nt(message.astype(BF16), places).astype(BF16)
        return nn(puts, jnp.concatenate([apart[:, 0:WIDE], apart[:, WIDE:]], axis=0))

    send_a[...] = pack(nn(pick_cols, inner))
    exchange(10, send_a, recv_a, plain)

    def projected(group):
        total = own[group]
        for k in range(1, TEAM):
            part_copy(group, k).wait_recv()
            total = total + part_in[group, k - 1].astype(F32)
        return total.astype(BF16)

    aug[0, 0:GROUP, :] = projected(0)
    place_lane = iota((16, LEN), 1)
    token_lane = token_of(place_lane)
    aug[0, GROUP : GROUP + 16, :] = jnp.where((token_lane >= first) & (token_lane < first + width), 1.0, 0.0).astype(BF16)
    send_b[...] = pack(nt(pick_cols, aug[0]))
    exchange(11, send_b, recv_b, plain)

    aug[1, 0:GROUP, :] = projected(1)
    identity = one_hot((LEN, LEN), lambda r, c: r == c)
    sub = iota((8, WIDE), 0)

    def prepare(pair, features, inner_b, mask_b):
        proj[pair] = features
        pre = nn(features[:, 0:LEN].astype(BF16), dtw[1 - pair])
        for second in range(2):
            d = 2 * second + pair
            v = pre[:, WIDE * second : WIDE * second + WIDE].astype(BF16).astype(F32) + bias[d : d + 1, :]
            size = mask_b * (jnp.maximum(v, 0.0) + jnp.log1p(jnp.exp(-jnp.abs(v))))
            step[d] = size
            drive[d] = size * inner_b

    def at(q, second):
        p = STEPS - 1 - q if second else q
        return pl.multiple_of(p * 8, 8)

    def gates(pair, second, rows):
        base = 2 * RANK + 2 * STATE * second
        tile = proj[pair, pl.ds(rows, 8), :]
        ins = [jnp.broadcast_to(tile[:, base + n : base + n + 1], (8, WIDE)) for n in range(STATE)]
        outs = [jnp.broadcast_to(tile[:, base + STATE + n : base + STATE + n + 1], (8, WIDE)) for n in range(STATE)]
        return ins, outs

    def roll_on(x, s, second, fill):
        moved = pltpu.roll(x, 8 - s if second else s, 0)
        keep = sub < 8 - s if second else sub >= s
        return jnp.where(keep, moved, fill)

    def totals(pair):
        part_states = STATE // 2
        zero = jnp.zeros((8, WIDE), F32)
        ends = {}
        for base in range(0, STATE, part_states):

            def advance(q, carry):
                new = []
                for second in range(2):
                    d, rows = 2 * second + pair, at(q, second)
                    size, push = step[d, pl.ds(rows, 8), :], drive[d, pl.ds(rows, 8), :]
                    tile = proj[pair, pl.ds(rows, 8), :]
                    lane = 2 * RANK + 2 * STATE * second + base
                    for n in range(part_states):
                        now = jnp.exp2(decay[d, base + n : base + n + 1, :] * size)
                        gate_in = jnp.broadcast_to(tile[:, lane + n : lane + n + 1], (8, WIDE))
                        new.append(now * carry[part_states * second + n] + push * gate_in)
                return tuple(new)

            got = lax.fori_loop(0, STEPS, advance, (zero,) * (2 * part_states), unroll=16)
            for second in range(2):
                for n in range(part_states):
                    ends[second, base + n] = got[part_states * second + n]
        for second in range(2):
            d = 2 * second + pair
            chunk = step[d, 0:8, :]
            for q in range(1, STEPS):
                chunk = chunk + step[d, 8 * q : 8 * q + 8, :]
            run = chunk
            for s in (1, 2, 4):
                run = run + roll_on(run, s, second, 0.0)
            carry_p[d] = roll_on(run, 1, second, 0.0)
            end = 0 if second else 7
            for n in range(STATE):
                h, p = ends[second, n], jnp.exp2(decay[d, n : n + 1, :] * chunk)
                for s in (1, 2, 4):
                    h = p * roll_on(h, s, second, 0.0) + h
                    if s < 4:
                        p = p * roll_on(p, s, second, 1.0)
                hexc[d, 8 * n : 8 * n + 8, :] = roll_on(h, 1, second, 0.0)
                for half in range(2):
                    k = 32 * second + 16 * half + n
                    send_h[pair, k : k + 1, 0:LEN] = h[end : end + 1, LEN * half : LEN * half + LEN]
            whole = jnp.exp2(decay[d] * run[end : end + 1, :])
            for half in range(2):
                k = 32 * second + 16 * half
                send_h[pair, k : k + STATE, LEN : 2 * LEN] = whole[:, LEN * half : LEN * half + LEN]

    def place_in_order(source, owner):
        return jnp.where(owner < PEERS // 2, source, PEERS - 1 - source)

    def send_totals(pair):
        exchange(
            12 + pair, send_h.at[pair], recv_h.at[pair], lambda src, dst: (dst, place_in_order(src, dst))
        )

    def own_scan(pair):
        arrive(12 + pair)
        h, p = recv_h[pair, :, 0:LEN], recv_h[pair, :, LEN : 2 * LEN]
        row = iota((PEERS, LEN), 0)
        for s in (1, 2, 4, 8, 16, 32):
            keep = row >= s
            h = p * jnp.where(keep, pltpu.roll(h, s, 0), 0.0) + h
            if s < 32:
                p = p * jnp.where(keep, pltpu.roll(p, s, 0), 1.0)
        send_c[pair] = jnp.where(row >= 1, pltpu.roll(h, 1, 0), 0.0)
        exchange(
            14 + pair, send_c.at[pair], recv_c.at[pair], lambda src, dst: (place_in_order(dst, src), src)
        )

    def local_pass(pair):
        for second in range(2):
            d = 2 * second + pair

            def advance(q, carry):
                rows = at(q, second)
                size, push = step[d, pl.ds(rows, 8), :], drive[d, pl.ds(rows, 8), :]
                ins, outs = gates(pair, second, rows)
                since = carry[STATE] + size
                new, y = [], jnp.zeros((8, WIDE), F32)
                for n in range(STATE):
                    rate = decay[d, n : n + 1, :]
                    h = jnp.exp2(rate * size) * carry[n] + push * ins[n]
                    y = y + outs[n] * h
                    cc[d, pl.ds(rows * STATE + 8 * n, 8), :] = outs[n] * jnp.exp2(rate * since)
                    new.append(h)
                local[d, pl.ds(rows, 8), :] = y
                return tuple(new) + (since,)

            lax.fori_loop(
                0, STEPS, advance,
                tuple(hexc[d, 8 * n : 8 * n + 8, :] for n in range(STATE)) + (carry_p[d],),
            )

    def finish(pair, dst):
        arrive(14 + pair)

        def advance(p, _):
            rows = pl.multiple_of(p * 8, 8)
            for half in range(2):
                lanes = slice(LEN * half, LEN * half + LEN)
                sums = [local[pair, pl.ds(rows, 8), lanes], local[2 + pair, pl.ds(rows, 8), lanes], None, None]
                for n in range(STATE):
                    for second in range(2):
                        k = 32 * second + 16 * half + n
                        term = cc[2 * second + pair, pl.ds(rows * STATE + 8 * n, 8), lanes] * recv_c[pair, k : k + 1, :]
                        spot = (2 * n + second) % 4
                        sums[spot] = term if sums[spot] is None else sums[spot] + term
                dst[pl.ds(rows, 8), lanes] = (sums[0] + sums[1]) + (sums[2] + sums[3])
            return _

        lax.fori_loop(0, STEPS, advance, 0, unroll=8)

    inner_f = inner.astype(F32)
    prepare(0, nt(identity, aug[1]), inner_f, row_mask)
    totals(0)
    send_totals(0)

    arrive(10)
    col_inner = unpack(recv_a[...], put_rows)
    arrive(11)
    col_feat = unpack(recv_b[...], put_rows)
    prepare(1, col_feat, col_inner, jnp.broadcast_to(col_feat[:, GROUP : GROUP + 1], (LEN, WIDE)))
    totals(1)
    send_totals(1)
    local_pass(1)
    own_scan(1)
    own_scan(0)
    local_pass(0)
    finish(1, ycol)
    back = ycol[...].astype(BF16)
    send_y[...] = pack(nn(pick_rows, back))
    exchange(16, send_y, recv_y, plain)
    finish(0, yrow)
    natural = one_hot((LEN, LEN), lambda p, t: token_of(p) == t)
    base = yrow[...] + skips[0:1, :] * inner_s[...].astype(F32)
    high = base.astype(BF16)
    base = (tn(high, natural) + tn((base - high.astype(F32)).astype(BF16), natural))[0:CHAN]
    gated = silu(gate[...].astype(F32))
    spots = one_hot((PEERS, 2 * LEN), lambda j, m: (m & (LEN - 1)) == 2 * j + (m >> 7))
    arrive(16)
    back = recv_y[...].astype(BF16)
    spread = tn(back, spots)
    returned = spread[0:CHAN, 0:LEN] + spread[CHAN:PACK, LEN : 2 * LEN]
    out[...] = ((base + returned) * gated).astype(BF16)

    for copy in sent:
        copy.wait_send()
    for group in range(2):
        for k in range(1, TEAM):
            part_copy(group, k).wait_send()


def body(
    feats, gate_in, conv_weight, conv_bias, xproj_weight, dtproj_weight, dt_bias, a_log, skip_gain, row_start, row_len
):
    vmem = pl.BlockSpec(memory_space=pltpu.VMEM)
    hbm = pl.BlockSpec(memory_space=pltpu.HBM)
    inputs = [
        ((CHAN, LEN), BF16), ((CHAN, LEN), BF16), ((9, CHAN), F32), ((1, CHAN), F32), ((CHAN, 2 * GROUP), BF16),
        ((4, RANK, CHAN), BF16), ((4, CHAN), F32), ((4, STATE, CHAN), F32), ((4, CHAN), F32),
    ]
    scratch = [
        ((3, WIDE, LEN), BF16),
        ((16, WIDE), F32),
        ((2 * GROUP, WIDE), BF16),
        ((2, GROUP, LEN), BF16),
        ((2, TEAM - 1, GROUP, LEN), BF16),
        ((2, LEN, 2 * WIDE), BF16),
        ((8, WIDE), F32),
        ((4, STATE, WIDE), F32),
        ((8, WIDE), F32),
        ((2, WIDE, LEN), BF16),
        ((4, LEN, WIDE), F32),
        ((4, LEN, WIDE), F32),
        ((2, LEN, WIDE), F32),
        ((4, STATE * 8, WIDE), F32),
        ((4, LEN, WIDE), F32),
        ((4, LEN * STATE, WIDE), F32),
        ((4, 8, WIDE), F32),
        ((PEERS, PACK), F32), ((PEERS, PACK), F32),
        ((PEERS, PACK), F32), ((PEERS, PACK), F32),
        ((2, PEERS, WIDE), F32), ((2, PEERS, WIDE), F32),
        ((2, PEERS, LEN), F32), ((2, PEERS, LEN), F32),
        ((PEERS, PACK), F32), ((PEERS, PACK), F32),
        ((LEN, WIDE), BF16),
        ((LEN, WIDE), F32), ((LEN, WIDE), F32),
        ((8, PACK), F32),
    ]
    return pl.pallas_call(
        body_kernel,
        out_shape=pltpu.VMEM((CHAN, LEN), BF16),
        in_specs=[hbm] * 11,
        out_specs=vmem,
        scratch_shapes=[pltpu.VMEM(s, t) for s, t in inputs] + [pltpu.SMEM((1, 1), jnp.int32)] * 2
        + [pltpu.VMEM(s, t) for s, t in scratch]
        + [pltpu.SemaphoreType.DMA((17,)), pltpu.SemaphoreType.DMA((17,)), pltpu.SemaphoreType.DMA((11,))],
        compiler_params=pltpu.CompilerParams(
            collective_id=0, has_side_effects=True, vmem_limit_bytes=56 * 1024 * 1024
        ),
    )(
        feats, gate_in, conv_weight, conv_bias.reshape(1, CHAN), xproj_weight, dtproj_weight, dt_bias,
        jnp.swapaxes(a_log, 1, 2), skip_gain, row_start.reshape(1, 1), row_len.reshape(1, 1),
    )


def solution(mesh):
    in_specs = (
        P("chan", "tissue"),
        P("chan", "tissue"),
        P(None, "chan"),
        P("chan"),
        P("chan", None),
        P(None, None, "chan"),
        P(None, "chan"),
        P(None, "chan", None),
        P(None, "chan"),
        P("tissue"),
        P("tissue"),
    )
    return jax.shard_map(body, mesh=mesh, in_specs=in_specs, out_specs=P("chan", "tissue"), check_vma=False)
```

```python
import jax
import jax.numpy as jnp
from jax import lax
from jax.experimental import pallas as pl
from jax.experimental.pallas import tpu as pltpu
from jax.sharding import PartitionSpec as P

MESH = pl.DeviceIdType.MESH
F32 = jnp.float32
BF16 = jnp.bfloat16
PEERS = 64
TEAM = 4
LEN = 128
CHAN = 192
WIDE = 256
STATE = 16
RANK = 48
GROUP = 2 * (RANK + 2 * STATE)
PACK = 2 * CHAN
STEPS = 16
LOG2E = 1.4426950408889634


def nn(a, b):
    return lax.dot_general(a, b, (((1,), (0,)), ((), ())), preferred_element_type=F32)


def nt(a, b):
    return lax.dot_general(a, b, (((1,), (1,)), ((), ())), preferred_element_type=F32)


def tn(a, b):
    return lax.dot_general(a, b, (((0,), (0,)), ((), ())), preferred_element_type=F32)


def token_of(place):
    return (place & 7) * STEPS + (place >> 3)


def iota(shape, dim):
    return lax.broadcasted_iota(jnp.int32, shape, dim)


def one_hot(shape, equal):
    return jnp.where(equal(iota(shape, 0), iota(shape, 1)), 1.0, 0.0).astype(BF16)


def silu(v):
    return v / (1.0 + jnp.exp(-v))


def body_kernel(
    feats_hbm, gate_hbm, conv_w_hbm, conv_b_hbm, xproj_hbm, dtproj_hbm, dt_bias_hbm, a_log_hbm, skip_hbm, start_hbm, len_hbm,
    out,
    feats, gate, conv_w, conv_b, xproj, dtproj, dt_bias, a_log, skip, row_start, row_len,
    rows3, convp, xw, part, part_in, dtw, bias, decay, skips, aug,
    step, drive, proj, hexc, local, cc, carry_p,
    send_a, recv_a, send_b, recv_b, send_h, recv_h, send_c, recv_c, send_y, recv_y,
    inner_s, yrow, ycol, spare,
    ssem, rsem, isem,
):
    me = lax.axis_index("tissue")
    team = lax.axis_index("chan")

    barrier = pltpu.get_barrier_semaphore()

    plane, core = me >> 4, me & 1
    lines = [(((me >> 1) + dz) & 7) * 2 for dz in (4, 3, 5, 2, 6, 1, 7, 0)]

    def to_peers(act):
        def one(q, _):
            base = ((plane + 2 + (q >> 1) - (q & 1)) & 3) * 16
            for line in lines:
                for other in (1 - core, core):
                    act(base + line + other)
            return _

        lax.fori_loop(0, 3, one, 0)
        for line in lines:
            act(plane * 16 + line + 1 - core)
        for line in lines[:-1]:
            act(plane * 16 + line + core)

    to_peers(lambda peer: pl.semaphore_signal(barrier, inc=1, device_id=(peer, team), device_id_type=MESH))
    for k in (2, 1, 3):
        pl.semaphore_signal(barrier, inc=1, device_id=(me, lax.rem(team + k, TEAM)), device_id_type=MESH)

    loads = [
        pltpu.make_async_copy(src, dst, isem.at[n])
        for n, (src, dst) in enumerate((
            (start_hbm, row_start), (len_hbm, row_len), (feats_hbm, feats), (xproj_hbm, xproj), (conv_w_hbm, conv_w),
            (conv_b_hbm, conv_b), (dtproj_hbm, dtproj), (dt_bias_hbm, dt_bias), (a_log_hbm, a_log), (skip_hbm, skip),
            (gate_hbm, gate),
        ))
    ]
    for load in loads:
        load.start()
    rows3[:, CHAN:, :] = jnp.zeros((3, WIDE - CHAN, LEN), BF16)
    for load in loads:
        load.wait()

    first, width = row_start[0, 0], row_len[0, 0]
    cols = iota((CHAN, LEN), 1)
    lane_mask = (cols >= first) & (cols < first + width)
    rows3[1, 0:CHAN, :] = jnp.where(lane_mask, feats[...], jnp.zeros((), BF16))

    shifts = one_hot((3 * LEN, LEN), lambda r, t: t == token_of(r & (LEN - 1)) + (r >> 7) - 1)
    convp[...] = jnp.zeros_like(convp)
    convp[0:9, 0:CHAN] = conv_w[...]
    convp[9:10, 0:CHAN] = conv_b[...]
    bias[...] = jnp.zeros_like(bias)
    bias[0:4, 0:CHAN] = dt_bias[...]
    skips[...] = jnp.zeros_like(skips)
    skips[0:1, 0:CHAN] = jnp.sum(skip[...], axis=0, keepdims=True)
    aug[...] = jnp.zeros_like(aug)

    turned = nt(one_hot((2 * GROUP, 2 * GROUP), lambda r, f: r == f), xproj[...]).astype(BF16)
    xw[...] = jnp.zeros_like(xw)
    for d in range(4):
        top, start = GROUP * (1 - d % 2), (RANK + 2 * STATE) * d
        low, gat = top + RANK * (d // 2), top + 2 * RANK + 2 * STATE * (d // 2)
        xw[low : low + RANK, 0:CHAN] = turned[start : start + RANK]
        xw[gat : gat + 2 * STATE, 0:CHAN] = turned[start + RANK : start + RANK + 2 * STATE]

    dtw[...] = jnp.zeros_like(dtw)
    for d in range(4):
        pair, second = 1 - d % 2, d // 2
        dtw[pair, RANK * second : RANK * second + RANK, WIDE * second : WIDE * second + CHAN] = dtproj[d]
    decay[...] = jnp.zeros_like(decay)
    for d in range(4):
        decay[d, :, 0:CHAN] = -LOG2E * jnp.exp(a_log[d])

    pl.semaphore_wait(barrier, PEERS - 1 + TEAM - 1)

    below = lax.rem(me + 1, PEERS)
    above = lax.rem(me + PEERS - 1, PEERS)
    halo = [
        pltpu.make_async_remote_copy(
            src_ref=rows3.at[1, pl.ds(0, CHAN)], dst_ref=rows3.at[slot, pl.ds(0, CHAN)],
            send_sem=ssem.at[slot], recv_sem=rsem.at[slot], device_id=(peer, team), device_id_type=MESH,
        )
        for slot, peer in ((0, below), (2, above))
    ]
    for copy in halo:
        copy.start()

    def conv_terms(i, source):
        x = nt(shifts, source)
        total = None
        for j in range(3):
            term = convp[3 * i + j : 3 * i + j + 1, :] * x[j * LEN : (j + 1) * LEN]
            total = term if total is None else total + term
        return total

    conv_sum = convp[9:10, :] + conv_terms(1, rows3[1])
    token_rows = token_of(iota((LEN, WIDE), 0))
    row_mask = jnp.where((token_rows >= first) & (token_rows < first + width), 1.0, 0.0)

    halo[0].wait_recv()
    conv_sum = conv_sum + jnp.where(me > 0, 1.0, 0.0) * conv_terms(0, rows3[0])
    halo[1].wait_recv()
    conv_sum = conv_sum + jnp.where(me < PEERS - 1, 1.0, 0.0) * conv_terms(2, rows3[2])
    inner = (silu(conv_sum) * row_mask).astype(BF16)
    inner_s[...] = inner

    def part_copy(group, k):
        sem = 4 + 3 * group + k - 1
        return pltpu.make_async_remote_copy(
            src_ref=part.at[group], dst_ref=part_in.at[group, k - 1],
            send_sem=ssem.at[sem], recv_sem=rsem.at[sem],
            device_id=(me, lax.rem(team + k, TEAM)), device_id_type=MESH,
        )

    own = []

    def send_part(group):
        own.append(nt(xw[group * GROUP : (group + 1) * GROUP, :], inner))
        part[group] = own[group].astype(BF16)
        for k in (2, 1, 3):
            part_copy(group, k).start()

    send_part(0)

    def exchange(sem, src, dst, slot_there):
        def send(peer):
            here, there = slot_there(me, peer)
            pltpu.make_async_remote_copy(
                src_ref=src.at[pl.ds(here, 1)], dst_ref=dst.at[pl.ds(there, 1)],
                send_sem=ssem.at[sem], recv_sem=rsem.at[sem], device_id=(peer, team), device_id_type=MESH,
            ).start()

        to_peers(send)
        here, there = slot_there(me, me)
        own_row = src.at[pl.ds(here, 1)]
        pltpu.make_async_copy(own_row, dst.at[pl.ds(there, 1)], rsem.at[sem]).start()
        pltpu.make_async_copy(own_row, spare.at[pl.ds(sem - 10, 1), pl.ds(0, src.shape[1])], ssem.at[sem]).start()
        due[sem] = all_rows(sem, src, dst)
        sent.append(due[sem])

    def arrive(sem):
        due.pop(sem).wait_recv()

    sent = list(halo)
    due = {}

    def all_rows(sem, src, dst):
        return pltpu.make_async_remote_copy(
            src_ref=src, dst_ref=dst,
            send_sem=ssem.at[sem], recv_sem=rsem.at[sem], device_id=(below, team), device_id_type=MESH,
        )

    plain = lambda src, dst: (dst, src)

    places = one_hot(
        (2 * WIDE, PACK), lambda e, l: (l == CHAN * (e >> 8) + (e & (WIDE - 1))) & ((e & (WIDE - 1)) < CHAN)
    )
    pick_cols = one_hot((LEN, LEN), lambda m, p: token_of(p) == 2 * (m & (PEERS - 1)) + (m >> 6))
    pick_rows = one_hot((LEN, LEN), lambda m, p: token_of(p) == m)
    put_rows = one_hot((LEN, LEN), lambda p, m: token_of(p) == m)

    def pack(picked):
        picked = picked.astype(BF16)
        return nn(picked[0:PEERS], places[0:WIDE]) + nn(picked[PEERS:], places[WIDE:])

    def unpack(message, puts):
        apart = nt(message.astype(BF16), places).astype(BF16)
        return nn(puts, jnp.concatenate([apart[:, 0:WIDE], apart[:, WIDE:]], axis=0))

    send_a[...] = pack(nn(pick_cols, inner))
    exchange(10, send_a, recv_a, plain)

    def projected(group):
        total = own[group]
        for k in range(1, TEAM):
            part_copy(group, k).wait_recv()
            total = total + part_in[group, k - 1].astype(F32)
        return total.astype(BF16)

    aug[0, 0:GROUP, :] = projected(0)
    place_lane = iota((16, LEN), 1)
    token_lane = token_of(place_lane)
    aug[0, GROUP : GROUP + 16, :] = jnp.where((token_lane >= first) & (token_lane < first + width), 1.0, 0.0).astype(BF16)
    send_b[...] = pack(nt(pick_cols, aug[0]))
    exchange(11, send_b, recv_b, plain)
    send_part(1)

    aug[1, 0:GROUP, :] = projected(1)
    identity = one_hot((LEN, LEN), lambda r, c: r == c)
    sub = iota((8, WIDE), 0)

    def prepare(pair, features, inner_b, mask_b):
        proj[pair] = features
        pre = nn(features[:, 0:LEN].astype(BF16), dtw[1 - pair])
        for second in range(2):
            d = 2 * second + pair
            v = pre[:, WIDE * second : WIDE * second + WIDE].astype(BF16).astype(F32) + bias[d : d + 1, :]
            size = mask_b * (jnp.maximum(v, 0.0) + jnp.log1p(jnp.exp(-jnp.abs(v))))
            step[d] = size
            drive[d] = size * inner_b

    def at(q, second):
        p = STEPS - 1 - q if second else q
        return pl.multiple_of(p * 8, 8)

    def gates(pair, second, rows):
        base = 2 * RANK + 2 * STATE * second
        tile = proj[pair, pl.ds(rows, 8), :]
        ins = [jnp.broadcast_to(tile[:, base + n : base + n + 1], (8, WIDE)) for n in range(STATE)]
        outs = [jnp.broadcast_to(tile[:, base + STATE + n : base + STATE + n + 1], (8, WIDE)) for n in range(STATE)]
        return ins, outs

    def roll_on(x, s, second, fill):
        moved = pltpu.roll(x, 8 - s if second else s, 0)
        keep = sub < 8 - s if second else sub >= s
        return jnp.where(keep, moved, fill)

    def totals(pair):
        part_states = STATE // 2
        zero = jnp.zeros((8, WIDE), F32)
        ends = {}
        for base in range(0, STATE, part_states):

            def advance(q, carry):
                new = []
                for second in range(2):
                    d, rows = 2 * second + pair, at(q, second)
                    size, push = step[d, pl.ds(rows, 8), :], drive[d, pl.ds(rows, 8), :]
                    tile = proj[pair, pl.ds(rows, 8), :]
                    lane = 2 * RANK + 2 * STATE * second + base
                    for n in range(part_states):
                        now = jnp.exp2(decay[d, base + n : base + n + 1, :] * size)
                        gate_in = jnp.broadcast_to(tile[:, lane + n : lane + n + 1], (8, WIDE))
                        new.append(now * carry[part_states * second + n] + push * gate_in)
                return tuple(new)

            got = lax.fori_loop(0, STEPS, advance, (zero,) * (2 * part_states), unroll=16)
            for second in range(2):
                for n in range(part_states):
                    ends[second, base + n] = got[part_states * second + n]
        for second in range(2):
            d = 2 * second + pair
            chunk = step[d, 0:8, :]
            for q in range(1, STEPS):
                chunk = chunk + step[d, 8 * q : 8 * q + 8, :]
            run = chunk
            for s in (1, 2, 4):
                run = run + roll_on(run, s, second, 0.0)
            carry_p[d] = roll_on(run, 1, second, 0.0)
            end = 0 if second else 7
            for n in range(STATE):
                h, p = ends[second, n], jnp.exp2(decay[d, n : n + 1, :] * chunk)
                for s in (1, 2, 4):
                    h = p * roll_on(h, s, second, 0.0) + h
                    if s < 4:
                        p = p * roll_on(p, s, second, 1.0)
                hexc[d, 8 * n : 8 * n + 8, :] = roll_on(h, 1, second, 0.0)
                for half in range(2):
                    k = 32 * second + 16 * half + n
                    send_h[pair, k : k + 1, 0:LEN] = h[end : end + 1, LEN * half : LEN * half + LEN]
            whole = jnp.exp2(decay[d] * run[end : end + 1, :])
            for half in range(2):
                k = 32 * second + 16 * half
                send_h[pair, k : k + STATE, LEN : 2 * LEN] = whole[:, LEN * half : LEN * half + LEN]

    def place_in_order(source, owner):
        return jnp.where(owner < PEERS // 2, source, PEERS - 1 - source)

    def send_totals(pair):
        exchange(
            12 + pair, send_h.at[pair], recv_h.at[pair], lambda src, dst: (dst, place_in_order(src, dst))
        )

    def own_scan(pair):
        arrive(12 + pair)
        h, p = recv_h[pair, :, 0:LEN], recv_h[pair, :, LEN : 2 * LEN]
        row = iota((PEERS, LEN), 0)
        for s in (1, 2, 4, 8, 16, 32):
            keep = row >= s
            h = p * jnp.where(keep, pltpu.roll(h, s, 0), 0.0) + h
            if s < 32:
                p = p * jnp.where(keep, pltpu.roll(p, s, 0), 1.0)
        send_c[pair] = jnp.where(row >= 1, pltpu.roll(h, 1, 0), 0.0)
        exchange(
            14 + pair, send_c.at[pair], recv_c.at[pair], lambda src, dst: (place_in_order(dst, src), src)
        )

    def local_pass(pair):
        for second in range(2):
            d = 2 * second + pair

            def advance(q, carry):
                rows = at(q, second)
                size, push = step[d, pl.ds(rows, 8), :], drive[d, pl.ds(rows, 8), :]
                ins, outs = gates(pair, second, rows)
                since = carry[STATE] + size
                new, y = [], jnp.zeros((8, WIDE), F32)
                for n in range(STATE):
                    rate = decay[d, n : n + 1, :]
                    h = jnp.exp2(rate * size) * carry[n] + push * ins[n]
                    y = y + outs[n] * h
                    cc[d, pl.ds(rows * STATE + 8 * n, 8), :] = outs[n] * jnp.exp2(rate * since)
                    new.append(h)
                local[d, pl.ds(rows, 8), :] = y
                return tuple(new) + (since,)

            lax.fori_loop(
                0, STEPS, advance,
                tuple(hexc[d, 8 * n : 8 * n + 8, :] for n in range(STATE)) + (carry_p[d],),
            )

    def finish(pair, dst):
        arrive(14 + pair)

        def advance(p, _):
            rows = pl.multiple_of(p * 8, 8)
            for half in range(2):
                lanes = slice(LEN * half, LEN * half + LEN)
                sums = [local[pair, pl.ds(rows, 8), lanes], local[2 + pair, pl.ds(rows, 8), lanes], None, None]
                for n in range(STATE):
                    for second in range(2):
                        k = 32 * second + 16 * half + n
                        term = cc[2 * second + pair, pl.ds(rows * STATE + 8 * n, 8), lanes] * recv_c[pair, k : k + 1, :]
                        spot = (2 * n + second) % 4
                        sums[spot] = term if sums[spot] is None else sums[spot] + term
                dst[pl.ds(rows, 8), lanes] = (sums[0] + sums[1]) + (sums[2] + sums[3])
            return _

        lax.fori_loop(0, STEPS, advance, 0, unroll=8)

    inner_f = inner.astype(F32)
    prepare(0, nt(identity, aug[1]), inner_f, row_mask)
    totals(0)
    send_totals(0)

    arrive(10)
    col_inner = unpack(recv_a[...], put_rows)
    arrive(11)
    col_feat = unpack(recv_b[...], put_rows)
    prepare(1, col_feat, col_inner, jnp.broadcast_to(col_feat[:, GROUP : GROUP + 1], (LEN, WIDE)))
    totals(1)
    send_totals(1)
    local_pass(1)
    own_scan(1)
    own_scan(0)
    local_pass(0)
    finish(1, ycol)
    back = ycol[...].astype(BF16)
    send_y[...] = pack(nn(pick_rows, back))
    exchange(16, send_y, recv_y, plain)
    finish(0, yrow)
    natural = one_hot((LEN, LEN), lambda p, t: token_of(p) == t)
    base = yrow[...] + skips[0:1, :] * inner_s[...].astype(F32)
    high = base.astype(BF16)
    base = (tn(high, natural) + tn((base - high.astype(F32)).astype(BF16), natural))[0:CHAN]
    gated = silu(gate[...].astype(F32))
    spots = one_hot((PEERS, 2 * LEN), lambda j, m: (m & (LEN - 1)) == 2 * j + (m >> 7))
    arrive(16)
    back = recv_y[...].astype(BF16)
    spread = tn(back, spots)
    returned = spread[0:CHAN, 0:LEN] + spread[CHAN:PACK, LEN : 2 * LEN]
    out[...] = ((base + returned) * gated).astype(BF16)

    for copy in sent:
        copy.wait_send()
    for group in range(2):
        for k in range(1, TEAM):
            part_copy(group, k).wait_send()


def body(
    feats, gate_in, conv_weight, conv_bias, xproj_weight, dtproj_weight, dt_bias, a_log, skip_gain, row_start, row_len
):
    vmem = pl.BlockSpec(memory_space=pltpu.VMEM)
    hbm = pl.BlockSpec(memory_space=pltpu.HBM)
    inputs = [
        ((CHAN, LEN), BF16), ((CHAN, LEN), BF16), ((9, CHAN), F32), ((1, CHAN), F32), ((CHAN, 2 * GROUP), BF16),
        ((4, RANK, CHAN), BF16), ((4, CHAN), F32), ((4, STATE, CHAN), F32), ((4, CHAN), F32),
    ]
    scratch = [
        ((3, WIDE, LEN), BF16),
        ((16, WIDE), F32),
        ((2 * GROUP, WIDE), BF16),
        ((2, GROUP, LEN), BF16),
        ((2, TEAM - 1, GROUP, LEN), BF16),
        ((2, LEN, 2 * WIDE), BF16),
        ((8, WIDE), F32),
        ((4, STATE, WIDE), F32),
        ((8, WIDE), F32),
        ((2, WIDE, LEN), BF16),
        ((4, LEN, WIDE), F32),
        ((4, LEN, WIDE), F32),
        ((2, LEN, WIDE), F32),
        ((4, STATE * 8, WIDE), F32),
        ((4, LEN, WIDE), F32),
        ((4, LEN * STATE, WIDE), F32),
        ((4, 8, WIDE), F32),
        ((PEERS, PACK), F32), ((PEERS, PACK), F32),
        ((PEERS, PACK), F32), ((PEERS, PACK), F32),
        ((2, PEERS, WIDE), F32), ((2, PEERS, WIDE), F32),
        ((2, PEERS, LEN), F32), ((2, PEERS, LEN), F32),
        ((PEERS, PACK), F32), ((PEERS, PACK), F32),
        ((LEN, WIDE), BF16),
        ((LEN, WIDE), F32), ((LEN, WIDE), F32),
        ((8, PACK), F32),
    ]
    return pl.pallas_call(
        body_kernel,
        out_shape=pltpu.VMEM((CHAN, LEN), BF16),
        in_specs=[hbm] * 11,
        out_specs=vmem,
        scratch_shapes=[pltpu.VMEM(s, t) for s, t in inputs] + [pltpu.SMEM((1, 1), jnp.int32)] * 2
        + [pltpu.VMEM(s, t) for s, t in scratch]
        + [pltpu.SemaphoreType.DMA((17,)), pltpu.SemaphoreType.DMA((17,)), pltpu.SemaphoreType.DMA((11,))],
        compiler_params=pltpu.CompilerParams(
            collective_id=0, has_side_effects=True, vmem_limit_bytes=56 * 1024 * 1024
        ),
    )(
        feats, gate_in, conv_weight, conv_bias.reshape(1, CHAN), xproj_weight, dtproj_weight, dt_bias,
        jnp.swapaxes(a_log, 1, 2), skip_gain, row_start.reshape(1, 1), row_len.reshape(1, 1),
    )


def solution(mesh):
    in_specs = (
        P("chan", "tissue"),
        P("chan", "tissue"),
        P(None, "chan"),
        P("chan"),
        P("chan", None),
        P(None, None, "chan"),
        P(None, "chan"),
        P(None, "chan", None),
        P(None, "chan"),
        P("tissue"),
        P("tissue"),
    )
    return jax.shard_map(body, mesh=mesh, in_specs=in_specs, out_specs=P("chan", "tissue"), check_vma=False)
```

```python
import jax
import jax.numpy as jnp
from jax import lax
from jax.experimental import pallas as pl
from jax.experimental.pallas import tpu as pltpu
from jax.sharding import PartitionSpec as P

MESH = pl.DeviceIdType.MESH
F32 = jnp.float32
BF16 = jnp.bfloat16
PEERS = 64
TEAM = 4
LEN = 128
CHAN = 192
WIDE = 256
STATE = 16
RANK = 48
GROUP = 2 * (RANK + 2 * STATE)
PACK = 2 * CHAN
STEPS = 16
LOG2E = 1.4426950408889634


def nn(a, b):
    return lax.dot_general(a, b, (((1,), (0,)), ((), ())), preferred_element_type=F32)


def nt(a, b):
    return lax.dot_general(a, b, (((1,), (1,)), ((), ())), preferred_element_type=F32)


def tn(a, b):
    return lax.dot_general(a, b, (((0,), (0,)), ((), ())), preferred_element_type=F32)


def token_of(place):
    return (place & 7) * STEPS + (place >> 3)


def iota(shape, dim):
    return lax.broadcasted_iota(jnp.int32, shape, dim)


def one_hot(shape, equal):
    return jnp.where(equal(iota(shape, 0), iota(shape, 1)), 1.0, 0.0).astype(BF16)


def silu(v):
    return v / (1.0 + jnp.exp(-v))


def body_kernel(
    feats_hbm, gate_hbm, conv_w_hbm, conv_b_hbm, xproj_hbm, dtproj_hbm, dt_bias_hbm, a_log_hbm, skip_hbm, start_hbm, len_hbm,
    out,
    feats, gate, conv_w, conv_b, xproj, dtproj, dt_bias, a_log, skip, row_start, row_len,
    rows3, convp, xw, part, part_in, dtw, bias, decay, skips, aug,
    step, drive, proj, hexc, local, cc, carry_p,
    send_a, recv_a, send_b, recv_b, send_h, recv_h, send_c, recv_c, send_y, recv_y,
    inner_s, yrow, ycol, spare,
    ssem, rsem, isem,
):
    me = lax.axis_index("tissue")
    team = lax.axis_index("chan")

    barrier = pltpu.get_barrier_semaphore()

    plane, core = me >> 4, me & 1
    lines = [(((me >> 1) + dz) & 7) * 2 for dz in (4, 3, 5, 2, 6, 1, 7, 0)]

    def to_peers(act):
        def one(q, _):
            base = ((plane + 2 + (q >> 1) - (q & 1)) & 3) * 16
            for line in lines:
                for other in (1 - core, core):
                    act(base + line + other)
            return _

        lax.fori_loop(0, 3, one, 0)
        for line in lines:
            act(plane * 16 + line + 1 - core)
        for line in lines[:-1]:
            act(plane * 16 + line + core)

    to_peers(lambda peer: pl.semaphore_signal(barrier, inc=1, device_id=(peer, team), device_id_type=MESH))
    for k in (2, 1, 3):
        pl.semaphore_signal(barrier, inc=1, device_id=(me, lax.rem(team + k, TEAM)), device_id_type=MESH)

    loads = [
        pltpu.make_async_copy(src, dst, isem.at[n])
        for n, (src, dst) in enumerate((
            (start_hbm, row_start), (len_hbm, row_len), (feats_hbm, feats), (xproj_hbm, xproj), (conv_w_hbm, conv_w),
            (conv_b_hbm, conv_b), (dtproj_hbm, dtproj), (dt_bias_hbm, dt_bias), (a_log_hbm, a_log), (skip_hbm, skip),
            (gate_hbm, gate),
        ))
    ]
    for load in loads:
        load.start()
    rows3[:, CHAN:, :] = jnp.zeros((3, WIDE - CHAN, LEN), BF16)
    for load in loads:
        load.wait()

    first, width = row_start[0, 0], row_len[0, 0]
    cols = iota((CHAN, LEN), 1)
    lane_mask = (cols >= first) & (cols < first + width)
    rows3[1, 0:CHAN, :] = jnp.where(lane_mask, feats[...], jnp.zeros((), BF16))

    shifts = one_hot((3 * LEN, LEN), lambda r, t: t == token_of(r & (LEN - 1)) + (r >> 7) - 1)
    convp[...] = jnp.zeros_like(convp)
    convp[0:9, 0:CHAN] = conv_w[...]
    convp[9:10, 0:CHAN] = conv_b[...]
    bias[...] = jnp.zeros_like(bias)
    bias[0:4, 0:CHAN] = dt_bias[...]
    skips[...] = jnp.zeros_like(skips)
    skips[0:1, 0:CHAN] = jnp.sum(skip[...], axis=0, keepdims=True)
    aug[...] = jnp.zeros_like(aug)

    turned = nt(one_hot((2 * GROUP, 2 * GROUP), lambda r, f: r == f), xproj[...]).astype(BF16)
    xw[...] = jnp.zeros_like(xw)
    for d in range(4):
        top, start = GROUP * (1 - d % 2), (RANK + 2 * STATE) * d
        low, gat = top + RANK * (d // 2), top + 2 * RANK + 2 * STATE * (d // 2)
        xw[low : low + RANK, 0:CHAN] = turned[start : start + RANK]
        xw[gat : gat + 2 * STATE, 0:CHAN] = turned[start + RANK : start + RANK + 2 * STATE]

    dtw[...] = jnp.zeros_like(dtw)
    for d in range(4):
        pair, second = 1 - d % 2, d // 2
        dtw[pair, RANK * second : RANK * second + RANK, WIDE * second : WIDE * second + CHAN] = dtproj[d]
    decay[...] = jnp.zeros_like(decay)
    for d in range(4):
        decay[d, :, 0:CHAN] = -LOG2E * jnp.exp(a_log[d])

    pl.semaphore_wait(barrier, PEERS - 1 + TEAM - 1)

    below = lax.rem(me + 1, PEERS)
    above = lax.rem(me + PEERS - 1, PEERS)
    halo = [
        pltpu.make_async_remote_copy(
            src_ref=rows3.at[1, pl.ds(0, CHAN)], dst_ref=rows3.at[slot, pl.ds(0, CHAN)],
            send_sem=ssem.at[slot], recv_sem=rsem.at[slot], device_id=(peer, team), device_id_type=MESH,
        )
        for slot, peer in ((0, below), (2, above))
    ]
    for copy in halo:
        copy.start()

    def conv_terms(i, source):
        x = nt(shifts, source)
        total = None
        for j in range(3):
            term = convp[3 * i + j : 3 * i + j + 1, :] * x[j * LEN : (j + 1) * LEN]
            total = term if total is None else total + term
        return total

    conv_sum = convp[9:10, :] + conv_terms(1, rows3[1])
    token_rows = token_of(iota((LEN, WIDE), 0))
    row_mask = jnp.where((token_rows >= first) & (token_rows < first + width), 1.0, 0.0)

    halo[0].wait_recv()
    conv_sum = conv_sum + jnp.where(me > 0, 1.0, 0.0) * conv_terms(0, rows3[0])
    halo[1].wait_recv()
    conv_sum = conv_sum + jnp.where(me < PEERS - 1, 1.0, 0.0) * conv_terms(2, rows3[2])
    inner = (silu(conv_sum) * row_mask).astype(BF16)
    inner_s[...] = inner

    def part_copy(group, k):
        sem = 4 + 3 * group + k - 1
        return pltpu.make_async_remote_copy(
            src_ref=part.at[group], dst_ref=part_in.at[group, k - 1],
            send_sem=ssem.at[sem], recv_sem=rsem.at[sem],
            device_id=(me, lax.rem(team + k, TEAM)), device_id_type=MESH,
        )

    own = []

    def send_part(group):
        own.append(nt(xw[group * GROUP : (group + 1) * GROUP, :], inner))
        part[group] = own[group].astype(BF16)
        for k in (2, 1, 3):
            part_copy(group, k).start()

    send_part(0)

    def exchange(sem, src, dst, slot_there):
        def send(peer):
            here, there = slot_there(me, peer)
            pltpu.make_async_remote_copy(
                src_ref=src.at[pl.ds(here, 1)], dst_ref=dst.at[pl.ds(there, 1)],
                send_sem=ssem.at[sem], recv_sem=rsem.at[sem], device_id=(peer, team), device_id_type=MESH,
            ).start()

        to_peers(send)
        here, there = slot_there(me, me)
        own_row = src.at[pl.ds(here, 1)]
        pltpu.make_async_copy(own_row, dst.at[pl.ds(there, 1)], rsem.at[sem]).start()
        pltpu.make_async_copy(own_row, spare.at[pl.ds(sem - 10, 1), pl.ds(0, src.shape[1])], ssem.at[sem]).start()
        due[sem] = all_rows(sem, src, dst)
        sent.append(due[sem])

    def arrive(sem):
        due.pop(sem).wait_recv()

    sent = list(halo)
    due = {}

    def all_rows(sem, src, dst):
        return pltpu.make_async_remote_copy(
            src_ref=src, dst_ref=dst,
            send_sem=ssem.at[sem], recv_sem=rsem.at[sem], device_id=(below, team), device_id_type=MESH,
        )

    plain = lambda src, dst: (dst, src)

    places = one_hot(
        (2 * WIDE, PACK), lambda e, l: (l == CHAN * (e >> 8) + (e & (WIDE - 1))) & ((e & (WIDE - 1)) < CHAN)
    )
    pick_cols = one_hot((LEN, LEN), lambda m, p: token_of(p) == 2 * (m & (PEERS - 1)) + (m >> 6))
    pick_rows = one_hot((LEN, LEN), lambda m, p: token_of(p) == m)
    put_rows = one_hot((LEN, LEN), lambda p, m: token_of(p) == m)

    def pack(picked):
        picked = picked.astype(BF16)
        return nn(picked[0:PEERS], places[0:WIDE]) + nn(picked[PEERS:], places[WIDE:])

    def unpack(message, puts):
        apart = nt(message.astype(BF16), places).astype(BF16)
        return nn(puts, jnp.concatenate([apart[:, 0:WIDE], apart[:, WIDE:]], axis=0))

    send_a[...] = pack(nn(pick_cols, inner))
    exchange(10, send_a, recv_a, plain)

    def projected(group):
        total = own[group]
        for k in range(1, TEAM):
            part_copy(group, k).wait_recv()
            total = total + part_in[group, k - 1].astype(F32)
        return total.astype(BF16)

    aug[0, 0:GROUP, :] = projected(0)
    place_lane = iota((16, LEN), 1)
    token_lane = token_of(place_lane)
    aug[0, GROUP : GROUP + 16, :] = jnp.where((token_lane >= first) & (token_lane < first + width), 1.0, 0.0).astype(BF16)
    send_b[...] = pack(nt(pick_cols, aug[0]))
    exchange(11, send_b, recv_b, plain)
    send_part(1)

    identity = one_hot((LEN, LEN), lambda r, c: r == c)
    sub = iota((8, WIDE), 0)

    def prepare(pair, features, inner_b, mask_b):
        proj[pair] = features
        pre = nn(features[:, 0:LEN].astype(BF16), dtw[1 - pair])
        for second in range(2):
            d = 2 * second + pair
            v = pre[:, WIDE * second : WIDE * second + WIDE].astype(BF16).astype(F32) + bias[d : d + 1, :]
            size = mask_b * (jnp.maximum(v, 0.0) + jnp.log1p(jnp.exp(-jnp.abs(v))))
            step[d] = size
            drive[d] = size * inner_b

    def at(q, second):
        p = STEPS - 1 - q if second else q
        return pl.multiple_of(p * 8, 8)

    def gates(pair, second, rows):
        base = 2 * RANK + 2 * STATE * second
        tile = proj[pair, pl.ds(rows, 8), :]
        ins = [jnp.broadcast_to(tile[:, base + n : base + n + 1], (8, WIDE)) for n in range(STATE)]
        outs = [jnp.broadcast_to(tile[:, base + STATE + n : base + STATE + n + 1], (8, WIDE)) for n in range(STATE)]
        return ins, outs

    def roll_on(x, s, second, fill):
        moved = pltpu.roll(x, 8 - s if second else s, 0)
        keep = sub < 8 - s if second else sub >= s
        return jnp.where(keep, moved, fill)

    def totals(pair):
        part_states = STATE // 2
        zero = jnp.zeros((8, WIDE), F32)
        ends = {}
        for base in range(0, STATE, part_states):

            def advance(q, carry):
                new = []
                for second in range(2):
                    d, rows = 2 * second + pair, at(q, second)
                    size, push = step[d, pl.ds(rows, 8), :], drive[d, pl.ds(rows, 8), :]
                    tile = proj[pair, pl.ds(rows, 8), :]
                    lane = 2 * RANK + 2 * STATE * second + base
                    for n in range(part_states):
                        now = jnp.exp2(decay[d, base + n : base + n + 1, :] * size)
                        gate_in = jnp.broadcast_to(tile[:, lane + n : lane + n + 1], (8, WIDE))
                        new.append(now * carry[part_states * second + n] + push * gate_in)
                return tuple(new)

            got = lax.fori_loop(0, STEPS, advance, (zero,) * (2 * part_states), unroll=16)
            for second in range(2):
                for n in range(part_states):
                    ends[second, base + n] = got[part_states * second + n]
        for second in range(2):
            d = 2 * second + pair
            chunk = step[d, 0:8, :]
            for q in range(1, STEPS):
                chunk = chunk + step[d, 8 * q : 8 * q + 8, :]
            run = chunk
            for s in (1, 2, 4):
                run = run + roll_on(run, s, second, 0.0)
            carry_p[d] = roll_on(run, 1, second, 0.0)
            end = 0 if second else 7
            for n in range(STATE):
                h, p = ends[second, n], jnp.exp2(decay[d, n : n + 1, :] * chunk)
                for s in (1, 2, 4):
                    h = p * roll_on(h, s, second, 0.0) + h
                    if s < 4:
                        p = p * roll_on(p, s, second, 1.0)
                hexc[d, 8 * n : 8 * n + 8, :] = roll_on(h, 1, second, 0.0)
                for half in range(2):
                    k = 32 * second + 16 * half + n
                    send_h[pair, k : k + 1, 0:LEN] = h[end : end + 1, LEN * half : LEN * half + LEN]
            whole = jnp.exp2(decay[d] * run[end : end + 1, :])
            for half in range(2):
                k = 32 * second + 16 * half
                send_h[pair, k : k + STATE, LEN : 2 * LEN] = whole[:, LEN * half : LEN * half + LEN]

    def place_in_order(source, owner):
        return jnp.where(owner < PEERS // 2, source, PEERS - 1 - source)

    def send_totals(pair):
        exchange(
            12 + pair, send_h.at[pair], recv_h.at[pair], lambda src, dst: (dst, place_in_order(src, dst))
        )

    def own_scan(pair):
        arrive(12 + pair)
        h, p = recv_h[pair, :, 0:LEN], recv_h[pair, :, LEN : 2 * LEN]
        row = iota((PEERS, LEN), 0)
        for s in (1, 2, 4, 8, 16, 32):
            keep = row >= s
            h = p * jnp.where(keep, pltpu.roll(h, s, 0), 0.0) + h
            if s < 32:
                p = p * jnp.where(keep, pltpu.roll(p, s, 0), 1.0)
        send_c[pair] = jnp.where(row >= 1, pltpu.roll(h, 1, 0), 0.0)
        exchange(
            14 + pair, send_c.at[pair], recv_c.at[pair], lambda src, dst: (place_in_order(dst, src), src)
        )

    def local_pass(pair, seconds=(0, 1)):
        for second in seconds:
            d = 2 * second + pair

            def advance(q, carry):
                rows = at(q, second)
                size, push = step[d, pl.ds(rows, 8), :], drive[d, pl.ds(rows, 8), :]
                ins, outs = gates(pair, second, rows)
                since = carry[STATE] + size
                new, y = [], jnp.zeros((8, WIDE), F32)
                for n in range(STATE):
                    rate = decay[d, n : n + 1, :]
                    h = jnp.exp2(rate * size) * carry[n] + push * ins[n]
                    y = y + outs[n] * h
                    cc[d, pl.ds(rows * STATE + 8 * n, 8), :] = outs[n] * jnp.exp2(rate * since)
                    new.append(h)
                local[d, pl.ds(rows, 8), :] = y
                return tuple(new) + (since,)

            lax.fori_loop(
                0, STEPS, advance,
                tuple(hexc[d, 8 * n : 8 * n + 8, :] for n in range(STATE)) + (carry_p[d],),
            )

    def finish(pair, dst):
        arrive(14 + pair)

        def advance(p, _):
            rows = pl.multiple_of(p * 8, 8)
            for half in range(2):
                lanes = slice(LEN * half, LEN * half + LEN)
                sums = [local[pair, pl.ds(rows, 8), lanes], local[2 + pair, pl.ds(rows, 8), lanes], None, None]
                for n in range(STATE):
                    for second in range(2):
                        k = 32 * second + 16 * half + n
                        term = cc[2 * second + pair, pl.ds(rows * STATE + 8 * n, 8), lanes] * recv_c[pair, k : k + 1, :]
                        spot = (2 * n + second) % 4
                        sums[spot] = term if sums[spot] is None else sums[spot] + term
                dst[pl.ds(rows, 8), lanes] = (sums[0] + sums[1]) + (sums[2] + sums[3])
            return _

        lax.fori_loop(0, STEPS, advance, 0, unroll=8)

    inner_f = inner.astype(F32)

    arrive(10)
    col_inner = unpack(recv_a[...], put_rows)
    arrive(11)
    col_feat = unpack(recv_b[...], put_rows)
    prepare(1, col_feat, col_inner, jnp.broadcast_to(col_feat[:, GROUP : GROUP + 1], (LEN, WIDE)))
    totals(1)
    send_totals(1)
    aug[1, 0:GROUP, :] = projected(1)
    prepare(0, nt(identity, aug[1]), inner_f, row_mask)
    totals(0)
    send_totals(0)
    local_pass(1, (0,))
    own_scan(1)
    local_pass(1, (1,))
    own_scan(0)
    finish(1, ycol)
    back = ycol[...].astype(BF16)
    send_y[...] = pack(nn(pick_rows, back))
    exchange(16, send_y, recv_y, plain)
    local_pass(0)
    finish(0, yrow)
    natural = one_hot((LEN, LEN), lambda p, t: token_of(p) == t)
    base = yrow[...] + skips[0:1, :] * inner_s[...].astype(F32)
    high = base.astype(BF16)
    base = (tn(high, natural) + tn((base - high.astype(F32)).astype(BF16), natural))[0:CHAN]
    gated = silu(gate[...].astype(F32))
    spots = one_hot((PEERS, 2 * LEN), lambda j, m: (m & (LEN - 1)) == 2 * j + (m >> 7))
    arrive(16)
    back = recv_y[...].astype(BF16)
    spread = tn(back, spots)
    returned = spread[0:CHAN, 0:LEN] + spread[CHAN:PACK, LEN : 2 * LEN]
    out[...] = ((base + returned) * gated).astype(BF16)

    for copy in sent:
        copy.wait_send()
    for group in range(2):
        for k in range(1, TEAM):
            part_copy(group, k).wait_send()


def body(
    feats, gate_in, conv_weight, conv_bias, xproj_weight, dtproj_weight, dt_bias, a_log, skip_gain, row_start, row_len
):
    vmem = pl.BlockSpec(memory_space=pltpu.VMEM)
    hbm = pl.BlockSpec(memory_space=pltpu.HBM)
    inputs = [
        ((CHAN, LEN), BF16), ((CHAN, LEN), BF16), ((9, CHAN), F32), ((1, CHAN), F32), ((CHAN, 2 * GROUP), BF16),
        ((4, RANK, CHAN), BF16), ((4, CHAN), F32), ((4, STATE, CHAN), F32), ((4, CHAN), F32),
    ]
    scratch = [
        ((3, WIDE, LEN), BF16),
        ((16, WIDE), F32),
        ((2 * GROUP, WIDE), BF16),
        ((2, GROUP, LEN), BF16),
        ((2, TEAM - 1, GROUP, LEN), BF16),
        ((2, LEN, 2 * WIDE), BF16),
        ((8, WIDE), F32),
        ((4, STATE, WIDE), F32),
        ((8, WIDE), F32),
        ((2, WIDE, LEN), BF16),
        ((4, LEN, WIDE), F32),
        ((4, LEN, WIDE), F32),
        ((2, LEN, WIDE), F32),
        ((4, STATE * 8, WIDE), F32),
        ((4, LEN, WIDE), F32),
        ((4, LEN * STATE, WIDE), F32),
        ((4, 8, WIDE), F32),
        ((PEERS, PACK), F32), ((PEERS, PACK), F32),
        ((PEERS, PACK), F32), ((PEERS, PACK), F32),
        ((2, PEERS, WIDE), F32), ((2, PEERS, WIDE), F32),
        ((2, PEERS, LEN), F32), ((2, PEERS, LEN), F32),
        ((PEERS, PACK), F32), ((PEERS, PACK), F32),
        ((LEN, WIDE), BF16),
        ((LEN, WIDE), F32), ((LEN, WIDE), F32),
        ((8, PACK), F32),
    ]
    return pl.pallas_call(
        body_kernel,
        out_shape=pltpu.VMEM((CHAN, LEN), BF16),
        in_specs=[hbm] * 11,
        out_specs=vmem,
        scratch_shapes=[pltpu.VMEM(s, t) for s, t in inputs] + [pltpu.SMEM((1, 1), jnp.int32)] * 2
        + [pltpu.VMEM(s, t) for s, t in scratch]
        + [pltpu.SemaphoreType.DMA((17,)), pltpu.SemaphoreType.DMA((17,)), pltpu.SemaphoreType.DMA((11,))],
        compiler_params=pltpu.CompilerParams(
            collective_id=0, has_side_effects=True, vmem_limit_bytes=56 * 1024 * 1024
        ),
    )(
        feats, gate_in, conv_weight, conv_bias.reshape(1, CHAN), xproj_weight, dtproj_weight, dt_bias,
        jnp.swapaxes(a_log, 1, 2), skip_gain, row_start.reshape(1, 1), row_len.reshape(1, 1),
    )


def solution(mesh):
    in_specs = (
        P("chan", "tissue"),
        P("chan", "tissue"),
        P(None, "chan"),
        P("chan"),
        P("chan", None),
        P(None, None, "chan"),
        P(None, "chan"),
        P(None, "chan", None),
        P(None, "chan"),
        P("tissue"),
        P("tissue"),
    )
    return jax.shard_map(body, mesh=mesh, in_specs=in_specs, out_specs=P("chan", "tissue"), check_vma=False)
```
